256 devices in a mesh: blk: 64 (over z, y, core), lon: 4 (over x).
Axes of the slice: x: 4, y: 4, z: 8, core: 2. Of those that a mesh axis runs over, the one named last changes fastest.
Arguments:
- spectra: float32 [64, 4, 2, 2, 2, 16384], P(None, 'lon', None, None, None, 'blk'), may hold values from -0.046875 to 0.046875
- source_tiles: int32 [64, 32, 2], P('blk', 'lon'), may hold values from 0 to 63, as said below
- tap_shift: int32 [64, 32, 2], P('blk', 'lon'), may hold values from -448 to 448
- kernels: float32 [64, 32, 2, 128], P('blk', 'lon'), may hold values from -0.375 to 0.375
Outputs:
- unlensed: float32 [512, 2, 32768], P('blk', None, 'lon')
- lensed: float32 [512, 2, 32768], P('blk', None, 'lon')
The draws below stay inside these ranges and needn't reach their ends.
Inputs may be any that keep to these rules, and one draw needn't show every extreme that they name: `source_tiles`: each source tile lies at most one cycle tile away from its reader tile's cycle tile.
All inputs are finite; a program needn't handle non-finite values.
Results may differ from the reference program's by a relative error of at most 0.0003.
Values sent between devices are 32-bit elements; how exact they have to be, the bound alone decides.
A program may use at most 128 MiB of HBM per device.

```python
import math
import jax
import jax.numpy as jnp
from jax import lax

MMAX = 16384
CYCLE_PIXELS = 32768
ORDER_RADIX = 128
TAPS = 128
MAXSHIFT = 448
TROWS = 8
PTILE = 1024
NSRC = 2
RBLK = 8
CYCLES = 512
N_LON = 4


def draw_source_tiles(key, part):
    key = jax.random.fold_in(key, 11)
    tile_count = CYCLES // TROWS
    steps = jax.random.randint(key, (tile_count, CYCLE_PIXELS // PTILE, NSRC), -1, 2)
    own_tile = jnp.arange(tile_count, dtype=jnp.int32)[:, None, None]
    return jnp.clip(own_tile + steps, 0, tile_count - 1).astype(jnp.int32)


def draw_tap_shift(key, part):
    key = jax.random.fold_in(key, 23)
    key_values, key_upper, key_lower = jax.random.split(key, 3)
    array_shape = (CYCLES // TROWS, CYCLE_PIXELS // PTILE, NSRC)
    total = array_shape[0] * array_shape[1] * array_shape[2]
    values = jax.random.randint(key_values, (total,), -MAXSHIFT, MAXSHIFT + 1)
    upper_spot = jax.random.randint(key_upper, (), 0, total // 2)
    lower_spot = jax.random.randint(key_lower, (), total // 2, total)
    values = values.at[upper_spot].set(MAXSHIFT)
    values = values.at[lower_spot].set(-MAXSHIFT)
    return values.reshape(array_shape).astype(jnp.int32)


def level_of(rng, dims, cuts, low, high):
    factor_of, own = 1.0, jax.random.fold_in(rng, 6)
    for dim, shards_of in cuts:
        steps = jnp.exp(jax.random.uniform(jax.random.fold_in(own, dim), (shards_of,), jnp.float32, low / len(cuts), high / len(cuts)))
        factor_of = factor_of * jnp.repeat(steps, dims[dim] // shards_of).reshape([-1 if axis == dim else 1 for axis in range(len(dims))])
    return factor_of


def gaussian(stream_key, extent, deviation, bound, cuts=(), kind=jnp.bfloat16):
    gain = level_of(stream_key, extent, cuts, -0.22, 0.18) if cuts else 1.0
    values = jax.random.normal(stream_key, extent, jnp.float32) * deviation * gain
    return jnp.minimum(jnp.maximum(values, -bound), bound).astype(kind)


def setup_inputs(seed: int = 0) -> dict:
    keys = jax.random.split(jax.random.key(seed), 5)
    return {
        "spectra": gaussian(keys[0], (CYCLES // RBLK, N_LON, RBLK // N_LON, 2, 2, MMAX), MMAX ** -0.5, 0.046875, ((1, 4), (5, 64)), jnp.float32),
        "source_tiles": draw_source_tiles(jax.random.fold_in(keys[4], 71), 0),
        "tap_shift": draw_tap_shift(jax.random.fold_in(keys[4], 71), 0),
        "kernels": gaussian(keys[3], (CYCLES // TROWS, CYCLE_PIXELS // PTILE, NSRC, TAPS), (TAPS * NSRC) ** -0.5, 0.375, ((0, 64), (1, 4)), jnp.float32),
    }


HIGHEST = lax.Precision.HIGHEST


def phase_angles_grid(row_count, col_count, period, col_start):
    row_index = jnp.arange(row_count, dtype=jnp.int32)[:, None]
    col_index = (jnp.arange(col_count, dtype=jnp.int32) + col_start)[None, :]
    turns = (row_index * col_index) % period
    phase = turns.astype(jnp.float32) * jnp.float32(2.0 * math.pi / period)
    return jnp.cos(phase), jnp.sin(phase)


def synthesize_cycles(harmonic_spectrum, upper_order_start, upper_order_count):
    number_cycles = harmonic_spectrum.shape[0]
    upper_order_digit = harmonic_spectrum.shape[3] // ORDER_RADIX
    lower_pixel_digits = CYCLE_PIXELS // ORDER_RADIX
    spectrum_matrix = harmonic_spectrum.reshape(number_cycles, 2, 2, upper_order_digit, ORDER_RADIX)
    real_part = spectrum_matrix[:, :, 0]
    imag_part = spectrum_matrix[:, :, 1]
    cos_first, sin_first = phase_angles_grid(upper_order_digit, lower_pixel_digits, lower_pixel_digits, jnp.int32(0))
    first_real = jnp.einsum("rcab,aj->rcbj", real_part, cos_first, precision=HIGHEST) - jnp.einsum("rcab,aj->rcbj", imag_part, sin_first, precision=HIGHEST)
    first_imag = jnp.einsum("rcab,aj->rcbj", real_part, sin_first, precision=HIGHEST) + jnp.einsum("rcab,aj->rcbj", imag_part, cos_first, precision=HIGHEST)
    cosine_rotation, sine_rotation = phase_angles_grid(ORDER_RADIX, lower_pixel_digits, CYCLE_PIXELS, jnp.int32(0))
    twist_real = first_real * cosine_rotation - first_imag * sine_rotation
    twist_imag = first_real * sine_rotation + first_imag * cosine_rotation
    cosine_final, sine_final = phase_angles_grid(ORDER_RADIX, upper_order_count, ORDER_RADIX, upper_order_start)
    pixels = jnp.einsum("rcbj,bk->rckj", twist_real, cosine_final, precision=HIGHEST) - jnp.einsum("rcbj,bk->rckj", twist_imag, sine_final, precision=HIGHEST)
    return pixels.reshape(number_cycles, 2, upper_order_count * lower_pixel_digits)


def tile_values(grid, row_start, col_start, taps):
    width = taps.shape[0]
    block_start = (col_start // width).astype(jnp.int32)
    offset = (col_start - block_start * width).astype(jnp.int32)
    count = PTILE // width
    window = lax.dynamic_slice(grid, (row_start.astype(jnp.int32), jnp.int32(0), block_start, jnp.int32(0)), (TROWS, 2, count + 2, width))
    triple = jnp.concatenate([window[:, :, :-2], window[:, :, 1:-1], window[:, :, 2:]], axis=3)
    spread = jnp.concatenate([jnp.zeros((width,), taps.dtype), taps, jnp.zeros((2 * width + 1,), taps.dtype)])
    placed = lax.dynamic_slice(spread, (jnp.int32(width) - offset,), (3 * width + 1,))
    toeplitz = jnp.tile(placed, width)[: 3 * width * width].reshape(width, 3 * width)
    result = jnp.einsum("rcbu,qu->rcbq", triple, toeplitz, precision=HIGHEST)
    return result.reshape(TROWS, 2, PTILE)


def lens_band(extended, sources, shifts, kernels, tile_base, halo_cols):
    tile_rows, tile_cols, source_count = sources.shape
    width = kernels.shape[3]
    padded_band = jnp.concatenate([extended, jnp.zeros((extended.shape[0], 2, width), extended.dtype)], axis=2)
    grid = padded_band.reshape(extended.shape[0], 2, padded_band.shape[2] // width, width)
    row_start = (sources - tile_base) * TROWS + TROWS
    col_base = (jnp.arange(tile_cols, dtype=jnp.int32) * PTILE)[None, :, None]
    col_start = col_base + shifts - TAPS // 2 + halo_cols
    item_count = tile_rows * tile_cols * source_count
    values = jax.vmap(tile_values, in_axes=(None, 0, 0, 0))(grid, row_start.reshape(item_count), col_start.reshape(item_count), kernels.reshape(item_count, width))
    values = values.reshape(tile_rows, tile_cols, source_count, TROWS, 2, PTILE).sum(axis=2)
    values = values.transpose(0, 2, 3, 1, 4)
    return values.reshape(tile_rows * TROWS, 2, tile_cols * PTILE)


def reference(spectra, source_tiles, tap_shift, kernels):
    flattened_values = spectra.reshape(CYCLES, 2, 2, MMAX)
    unlensed = synthesize_cycles(flattened_values, jnp.int32(0), ORDER_RADIX)
    halo_cols = MAXSHIFT + TAPS // 2
    wide = jnp.concatenate([unlensed[:, :, CYCLE_PIXELS - halo_cols:], unlensed, unlensed[:, :, :halo_cols]], axis=2)
    border = jnp.zeros((TROWS, 2, wide.shape[2]), jnp.float32)
    extended = jnp.concatenate([border, wide, border], axis=0)

    def one_tile(items):
        sources, shifts, taps = items
        return lens_band(extended, sources[None], shifts[None], taps[None], jnp.int32(0), halo_cols)

    bands = lax.map(one_tile, (source_tiles, tap_shift, kernels))
    lensed = bands.reshape(CYCLES, 2, CYCLE_PIXELS)
    return unlensed, lensed
```

```python
import functools
import math

import jax
import jax.numpy as jnp
import ml_dtypes
import numpy as np
from jax import lax
from jax.experimental import pallas as pl
from jax.experimental.pallas import tpu as pltpu
from jax.sharding import PartitionSpec as P

NBLK = 64
NLON = 4
MESH = pl.DeviceIdType.MESH
F32 = jnp.float32
BF16 = jnp.bfloat16

ROWS = 72


def split(values):
    high = values.astype(ml_dtypes.bfloat16)
    low = (values - high.astype(np.float64)).astype(ml_dtypes.bfloat16)
    return high, low


def tables():
    def angle(rows, cols, period):
        return 2.0 * math.pi * ((rows[:, None] * cols[None, :]) % period) / period

    i = np.arange(128)
    b = np.arange(NBLK)
    n = np.arange(256)
    first = angle(i, b, 128)
    first = np.block([[np.cos(first), -np.sin(first)], [np.sin(first), np.cos(first)]])
    high, low = split(first)
    first = np.concatenate([high, low, high], axis=1)
    turn = angle(i, n, 32768)
    pixel_rows = np.concatenate([(64 * l + np.arange(ROWS) - 4) % 256 for l in range(NLON)])
    last = angle(pixel_rows, n, 256)
    last = np.concatenate([np.cos(last), -np.sin(last)], axis=1)
    last_high, last_low = split(last)
    return (
        first,
        np.cos(turn).astype(np.float32),
        np.sin(turn).astype(np.float32),
        last_high,
        last_low,
    )


def halves(x):
    high = x.astype(BF16)
    return high, (x - high.astype(F32)).astype(BF16)


def nt(a, b):
    return lax.dot_general(a, b, (((1,), (1,)), ((), ())), preferred_element_type=F32)


def synthesize(land, first_ref, cos_ref, sin_ref, high_ref, low_ref, made):
    for k in range(2):
        for q in range(2):
            kq = 2 * k + q
            parts = []
            for ri in range(2):
                rows = [land[pl.ds(4 * kq + 2 * h + ri, NBLK, stride=16), :] for h in range(2)]
                parts.append(jnp.concatenate(rows, axis=1))
            xh, xl = halves(jnp.concatenate(parts, axis=0))
            spread = jnp.concatenate([xh, xh, xl], axis=0)
            g = jnp.dot(first_ref[...], spread, preferred_element_type=F32)
            gre, gim = g[:128], g[128:]
            cos, sin = cos_ref[...], sin_ref[...]
            hh, hl = halves(
                jnp.concatenate([gre * cos - gim * sin, gre * sin + gim * cos], axis=1)
            )
            out = nt(high_ref[...], hh) + (nt(low_ref[...], hh) + nt(high_ref[...], hl))
            for l in range(NLON):
                made[l, k, pl.ds(q, ROWS, stride=2), :] = out[ROWS * l : ROWS * (l + 1)]


def lens(blk, src_ref, shift_ref, taps_ref, ext, lensed_ref):
    q_index = lax.broadcasted_iota(jnp.int32, (128, 128), 0)
    u_index = lax.broadcasted_iota(jnp.int32, (128, 128), 1)
    lead = u_index - q_index

    def one(g, carry):
        total = None
        for k in range(2):
            which = jnp.clip(src_ref[0, g, k] - blk + 1, 0, 2)
            start = shift_ref[0, g, k] + 448
            base = jnp.clip(lax.shift_right_arithmetic(start, 7), 0, 6)
            off = start - 128 * base
            taps = jnp.broadcast_to(taps_ref[pl.ds(2 * g + k, 1), :], (8, 128))
            taps = pltpu.roll(taps, off & 127, 1)
            ring = pltpu.roll(
                jnp.broadcast_to(taps[:1], (128, 128)), 0, 1, stride=1, stride_axis=0
            )
            toep = []
            wins = []
            for i in range(3):
                at = lead + (128 * i - off)
                toep.append(jnp.where((at >= 0) & (at < 128), ring, 0.0))
                row = 2 * (8 * g + base + i)
                wins.append(
                    jnp.concatenate(
                        [ext[which, u, pl.ds(row, 16), :] for u in range(8)], axis=0
                    )
                )
            th, tl = halves(jnp.concatenate(toep, axis=1))
            wh, wl = halves(jnp.concatenate(wins, axis=1))
            part = nt(wh, th) + (nt(wl, th) + nt(wh, tl))
            total = part if total is None else total + part
        for u in range(8):
            lensed_ref[u, pl.ds(pl.multiple_of(16 * g, 16), 16), :] = total[16 * u : 16 * u + 16]
        return carry

    lax.fori_loop(0, 8, one, 0)


def kernel(
    spec_ref, src_ref, shift_ref, taps_ref, first_ref, cos_ref, sin_ref, high_ref, low_ref,
    plain_ref, lensed_ref,
    land, made, ext, own_sem, send_a, recv_a, send_b, recv_b, send_c, recv_c,
):
    blk = lax.axis_index("blk")
    lon = lax.axis_index("lon")
    up = lax.rem(blk + 1, NBLK)
    down = lax.rem(blk + NBLK - 1, NBLK)

    barrier = pltpu.get_barrier_semaphore()

    def greet(o, carry):
        pl.semaphore_signal(
            barrier, inc=1, device_id=(lax.rem(blk + o, NBLK), lon), device_id_type=MESH
        )
        return carry

    lax.fori_loop(1, NBLK, greet, 0)
    for d in range(1, NLON):
        pl.semaphore_signal(
            barrier, inc=1, device_id=(blk, lax.rem(lon + d, NLON)), device_id_type=MESH
        )
    mine = pl.ds(pl.multiple_of(16 * blk, 16), 16)
    own = pltpu.make_async_copy(spec_ref.at[blk], land.at[mine], own_sem.at[0])
    own.start()
    pl.semaphore_wait(barrier, NBLK - 1 + NLON - 1)

    def send(o, carry):
        to = lax.rem(blk + o, NBLK)
        pltpu.make_async_remote_copy(
            src_ref=spec_ref.at[to],
            dst_ref=land.at[mine],
            send_sem=send_a,
            recv_sem=recv_a,
            device_id=(to, lon),
            device_id_type=MESH,
        ).start()
        return carry

    lax.fori_loop(1, NBLK, send, 0)
    own.wait()
    others = land.at[pl.ds(0, 16 * (NBLK - 1))]
    pltpu.make_async_copy(others, others, recv_a).wait()

    synthesize(land, first_ref, cos_ref, sin_ref, high_ref, low_ref, made)

    def across(d):
        to = lax.rem(lon + d, NLON)
        return pltpu.make_async_remote_copy(
            src_ref=made.at[to],
            dst_ref=ext.at[1, pl.ds(2 * lon, 2)],
            send_sem=send_b.at[d],
            recv_sem=recv_b.at[d],
            device_id=(blk, to),
            device_id_type=MESH,
        )

    def beside(d, source, l, to, slot, side):
        return pltpu.make_async_remote_copy(
            src_ref=source,
            dst_ref=ext.at[slot, pl.ds(2 * l, 2)],
            send_sem=send_c.at[side, d],
            recv_sem=recv_c.at[side, d],
            device_id=(to, lon),
            device_id_type=MESH,
        )

    sent_b = [across(d) for d in (1, 3, 2)]
    for copy in sent_b:
        copy.start()
    sent_c = []
    for d in (0, 1, 3, 2):
        l = lax.rem(lon + NLON - d, NLON)
        if d == 0:
            source = made.at[lon]
            keep = pltpu.make_async_copy(source, ext.at[1, pl.ds(2 * lon, 2)], own_sem.at[1])
            keep.start()
        else:
            across(d).wait_recv()
            source = ext.at[1, pl.ds(2 * l, 2)]
        for to, slot, side in ((up, 0, 0), (down, 2, 1)):
            copy = beside(d, source, l, to, slot, side)
            copy.start()
            sent_c.append(copy)
    keep.wait()
    plain_ref[...] = ext[1, :, 8:136, :]
    for copy in sent_c:
        copy.wait_recv()

    lens(blk, src_ref, shift_ref, taps_ref, ext, lensed_ref)

    pltpu.make_async_copy(others, others, send_a).wait()
    for copy in sent_b:
        copy.wait_send()
    for copy in sent_c:
        copy.wait_send()


def shards(spectra, source_tiles, tap_shift, kernels):
    spec = spectra.reshape(NBLK, 2, 2, 2, 2, 128).transpose(0, 1, 2, 4, 3, 5).reshape(NBLK, 16, 128)
    vmem = pl.BlockSpec(memory_space=pltpu.VMEM)
    smem = pl.BlockSpec(memory_space=pltpu.SMEM)
    shape = jax.ShapeDtypeStruct((8, 128, 128), F32)
    plain, lensed = pl.pallas_call(
        kernel,
        out_shape=(shape, shape),
        in_specs=[pl.BlockSpec(memory_space=pl.ANY), smem, smem] + [vmem] * 6,
        out_specs=(vmem, vmem),
        scratch_shapes=[
            pltpu.VMEM((16 * NBLK, 128), F32),
            pltpu.VMEM((NLON, 2, 2 * ROWS, 128), F32),
            pltpu.VMEM((3, 8, 2 * ROWS, 128), F32),
            pltpu.SemaphoreType.DMA((2,)),
            pltpu.SemaphoreType.DMA,
            pltpu.SemaphoreType.DMA,
            pltpu.SemaphoreType.DMA((NLON,)),
            pltpu.SemaphoreType.DMA((NLON,)),
            pltpu.SemaphoreType.DMA((2, NLON)),
            pltpu.SemaphoreType.DMA((2, NLON)),
        ],
        compiler_params=pltpu.CompilerParams(
            collective_id=0, has_side_effects=True, vmem_limit_bytes=40 * 1024 * 1024
        ),
    )(spec, source_tiles, tap_shift, kernels.reshape(16, 128), *map(jnp.asarray, tables()))

    def maps(x):
        return x.reshape(8, 64, 2, 128).transpose(0, 2, 1, 3).reshape(8, 2, 8192)

    return maps(plain), maps(lensed)


def solution(mesh):
    placed = (
        P(None, "lon", None, None, None, "blk"),
        P("blk", "lon", None),
        P("blk", "lon", None),
        P("blk", "lon", None, None),
    )
    return jax.shard_map(
        shards,
        mesh=mesh,
        in_specs=placed,
        out_specs=(P("blk", None, "lon"), P("blk", None, "lon")),
        check_vma=False,
    )
```

```python
import math

import jax
import jax.numpy as jnp
import numpy as np
from jax import lax
from jax.experimental import pallas as pl
from jax.experimental.pallas import tpu as pltpu
from jax.sharding import PartitionSpec as P

NBLK = 64
NLON = 4
STAGE = 4
MESH = pl.DeviceIdType.MESH
F32 = jnp.float32
BF16 = jnp.bfloat16

ROWS = 72


def tables():
    def angle(rows, cols, period):
        return 2.0 * math.pi * ((rows[:, None] * cols[None, :]) % period) / period

    i = np.arange(128)
    b = np.arange(NBLK)
    n = np.arange(256)
    first = angle(i, b, 128)
    first = np.block([[np.cos(first), -np.sin(first)], [np.sin(first), np.cos(first)]])
    turn = angle(i, n, 32768)
    pixel_rows = np.concatenate([(64 * l + np.arange(ROWS) - 4) % 256 for l in range(NLON)])
    last = angle(pixel_rows, n, 256)
    last = np.concatenate([np.cos(last), -np.sin(last)], axis=1)
    return tuple(t.astype(np.float32) for t in (first, np.cos(turn), np.sin(turn), last))


def halves(x):
    high = x.astype(BF16)
    return high, (x - high.astype(F32)).astype(BF16)


def nt(a, b):
    return lax.dot_general(a, b, (((1,), (1,)), ((), ())), preferred_element_type=F32)


def synthesize(land, first_ref, cos_ref, sin_ref, high_ref, low_ref, made):
    for k in range(2):
        for q in range(2):
            kq = 2 * k + q
            parts = []
            for ri in range(2):
                rows = [land[pl.ds(4 * kq + 2 * h + ri, NBLK, stride=16), :] for h in range(2)]
                parts.append(jnp.concatenate(rows, axis=1))
            xh, xl = halves(jnp.concatenate(parts, axis=0))
            spread = jnp.concatenate([xh, xh, xl], axis=0)
            g = jnp.dot(first_ref[...], spread, preferred_element_type=F32)
            gre, gim = g[:128], g[128:]
            cos, sin = cos_ref[...], sin_ref[...]
            hh, hl = halves(
                jnp.concatenate([gre * cos - gim * sin, gre * sin + gim * cos], axis=1)
            )
            out = nt(high_ref[...], hh) + (nt(low_ref[...], hh) + nt(high_ref[...], hl))
            for l in range(NLON):
                made[l, k, pl.ds(q, ROWS, stride=2), :] = out[ROWS * l : ROWS * (l + 1)]


def base_of(shift):
    start = shift + 448
    base = jnp.clip(lax.shift_right_arithmetic(start, 7), 0, 6)
    return base, start - 128 * base


def place_taps(shift_ref, taps_ref, toep):
    q_index = lax.broadcasted_iota(jnp.int32, (128, 128), 0)
    u_index = lax.broadcasted_iota(jnp.int32, (128, 128), 1)
    lead = u_index - q_index

    def one(g, carry):
        for k in range(2):
            _, off = base_of(shift_ref[k, g])
            taps = jnp.broadcast_to(taps_ref[pl.ds(2 * g + k, 1), :], (8, 128))
            taps = pltpu.roll(taps, off & 127, 1)
            ring = pltpu.roll(
                jnp.broadcast_to(taps[:1], (128, 128)), 0, 1, stride=1, stride_axis=0
            )
            high = ring.astype(BF16).astype(F32)
            low = ring - high
            for i in range(3):
                at = lead + (128 * i - off)
                keep = (at >= 0) & (at < 128)
                toep[2 * g + k, :, 128 * i : 128 * i + 128] = jnp.where(keep, high, 0.0).astype(BF16)
                toep[2 * g + k, :, 128 * i + 384 : 128 * i + 512] = jnp.where(
                    keep, low, 0.0
                ).astype(BF16)
        return carry

    lax.fori_loop(0, 8, one, 0)


def kernel(
    spec_ref, shift_hbm, taps_hbm, first_hbm, cos_hbm, sin_hbm, last_hbm,
    ext, toep,
    land, made, shift_ref, taps_ref, first_ref, cos_ref, sin_ref, last_ref, first_cat, high_ref, low_ref,
    own_sem, send_a, recv_a, send_b, recv_b, send_c, recv_c,
):
    blk = lax.axis_index("blk")
    lon = lax.axis_index("lon")
    up = lax.rem(blk + 1, NBLK)
    down = lax.rem(blk + NBLK - 1, NBLK)

    barrier = pltpu.get_barrier_semaphore()

    def greet(o, carry):
        pl.semaphore_signal(
            barrier, inc=1, device_id=(lax.rem(blk + o, NBLK), lon), device_id_type=MESH
        )
        return carry

    lax.fori_loop(1, NBLK, greet, 0)
    for d in range(1, NLON):
        pl.semaphore_signal(
            barrier, inc=1, device_id=(blk, lax.rem(lon + d, NLON)), device_id_type=MESH
        )
    mine = pl.ds(pl.multiple_of(16 * blk, 16), 16)
    loads = [
        pltpu.make_async_copy(source, target, own_sem.at[j])
        for j, (source, target) in enumerate(
            (
                (spec_ref.at[blk], land.at[mine]),
                (shift_hbm, shift_ref),
                (taps_hbm, taps_ref),
                (first_hbm, first_ref),
                (cos_hbm, cos_ref),
                (sin_hbm, sin_ref),
                (last_hbm, last_ref),
            )
        )
    ]
    for load in loads:
        load.start()
    pl.semaphore_wait(barrier, NBLK - 1 + NLON - 1)

    def send(o, carry):
        to = lax.rem(blk + o, NBLK)
        pltpu.make_async_remote_copy(
            src_ref=spec_ref.at[to],
            dst_ref=land.at[mine],
            send_sem=send_a,
            recv_sem=recv_a,
            device_id=(to, lon),
            device_id_type=MESH,
        ).start()
        return carry

    if STAGE >= 1:
        lax.fori_loop(1, NBLK, send, 0)
    for load in loads:
        load.wait()
    place_taps(shift_ref, taps_ref, toep)
    fh, fl = halves(first_ref[...])
    first_cat[...] = jnp.concatenate([fh, fl, fh], axis=1)
    lh, ll = halves(last_ref[...])
    high_ref[...] = lh
    low_ref[...] = ll

    others = land.at[pl.ds(0, 16 * (NBLK - 1))]
    if STAGE >= 1:
        pltpu.make_async_copy(others, others, recv_a).wait()

    if STAGE >= 2:
        synthesize(land, first_cat, cos_ref, sin_ref, high_ref, low_ref, made)

    def across(d):
        to = lax.rem(lon + d, NLON)
        return pltpu.make_async_remote_copy(
            src_ref=made.at[to],
            dst_ref=ext.at[1, pl.ds(2 * lon, 2)],
            send_sem=send_b.at[d],
            recv_sem=recv_b.at[d],
            device_id=(blk, to),
            device_id_type=MESH,
        )

    def beside(d, source, l, to, slot, side):
        return pltpu.make_async_remote_copy(
            src_ref=source,
            dst_ref=ext.at[slot, pl.ds(2 * l, 2)],
            send_sem=send_c.at[side, d],
            recv_sem=recv_c.at[side, d],
            device_id=(to, lon),
            device_id_type=MESH,
        )

    sent_b = [across(d) for d in (1, 3, 2)] if STAGE >= 3 else []
    for copy in sent_b:
        copy.start()
    sent_c = []
    for d in (0, 1, 3, 2):
        l = lax.rem(lon + NLON - d, NLON)
        if d == 0:
            source = made.at[lon]
            keep = pltpu.make_async_copy(source, ext.at[1, pl.ds(2 * lon, 2)], own_sem.at[7])
            keep.start()
        else:
            if STAGE >= 3:
                across(d).wait_recv()
            source = ext.at[1, pl.ds(2 * l, 2)]
        if STAGE < 4:
            continue
        for to, slot, side in ((up, 0, 0), (down, 2, 1)):
            copy = beside(d, source, l, to, slot, side)
            copy.start()
            sent_c.append(copy)
    keep.wait()
    for copy in sent_c:
        copy.wait_recv()
    if STAGE >= 1:
        pltpu.make_async_copy(others, others, send_a).wait()
    for copy in sent_b:
        copy.wait_send()
    for copy in sent_c:
        copy.wait_send()


def lens_kernel(
    src_hbm, shift_hbm, ext, toep, plain_ref, lensed_ref, src_ref, shift_ref, out, sems, out_sem
):
    blk = lax.axis_index("blk")
    loads = [
        pltpu.make_async_copy(src_hbm, src_ref, sems.at[0]),
        pltpu.make_async_copy(shift_hbm, shift_ref, sems.at[1]),
    ]
    for load in loads:
        load.start()
    keep = pltpu.make_async_copy(ext.at[1, :, pl.ds(8, 128), :], plain_ref, sems.at[2])
    keep.start()
    for load in loads:
        load.wait()
    copies = []
    for g in range(8):
        total = None
        for k in range(2):
            which = jnp.clip(src_ref[k, g] - blk + 1, 0, 2)
            base, _ = base_of(shift_ref[k, g])
            wins = []
            for i in range(3):
                row = 2 * (8 * g + base + i)
                wins.append(
                    jnp.concatenate(
                        [ext[which, u, pl.ds(row, 16), :] for u in range(8)], axis=0
                    )
                )
            wh, wl = halves(jnp.concatenate(wins, axis=1))
            th, tl = toep[2 * g + k, :, :384], toep[2 * g + k, :, 384:]
            part = nt(wh, th) + (nt(wl, th) + nt(wh, tl))
            total = part if total is None else total + part
        rows = pl.ds(16 * g, 16)
        out[:, rows, :] = total.reshape(8, 16, 128)
        copy = pltpu.make_async_copy(out.at[:, rows, :], lensed_ref.at[:, rows, :], out_sem.at[g])
        copy.start()
        copies.append(copy)
    keep.wait()
    for copy in copies:
        copy.wait()


def shards(spectra, source_tiles, tap_shift, kernels):
    spec = spectra.reshape(NBLK, 2, 2, 2, 2, 128).transpose(0, 1, 2, 4, 3, 5).reshape(NBLK, 16, 128)
    sources = source_tiles.transpose(0, 2, 1).reshape(2, 8)
    shifts = tap_shift.transpose(0, 2, 1).reshape(2, 8)
    vmem = pl.BlockSpec(memory_space=pltpu.VMEM)
    smem = pl.BlockSpec(memory_space=pltpu.SMEM)
    hbm = pl.BlockSpec(memory_space=pltpu.HBM)
    dma = pltpu.SemaphoreType.DMA
    ext, toep = pl.pallas_call(
        kernel,
        out_shape=(
            jax.ShapeDtypeStruct((3, 8, 2 * ROWS, 128), F32),
            jax.ShapeDtypeStruct((16, 128, 768), BF16),
        ),
        in_specs=[hbm] * 7,
        out_specs=(vmem, vmem),
        scratch_shapes=[
            pltpu.VMEM((16 * NBLK, 128), F32),
            pltpu.VMEM((NLON, 2, 2 * ROWS, 128), F32),
            pltpu.SMEM((2, 8), jnp.int32),
            pltpu.VMEM((16, 128), F32),
            pltpu.VMEM((256, 128), F32),
            pltpu.VMEM((128, 256), F32),
            pltpu.VMEM((128, 256), F32),
            pltpu.VMEM((NLON * ROWS, 512), F32),
            pltpu.VMEM((256, 384), BF16),
            pltpu.VMEM((NLON * ROWS, 512), BF16),
            pltpu.VMEM((NLON * ROWS, 512), BF16),
            dma((8,)),
            dma,
            dma,
            dma((NLON,)),
            dma((NLON,)),
            dma((2, NLON)),
            dma((2, NLON)),
        ],
        compiler_params=pltpu.CompilerParams(
            collective_id=0, has_side_effects=True, vmem_limit_bytes=32 * 1024 * 1024
        ),
    )(*(pltpu.with_memory_space_constraint(x, pltpu.HBM) for x in (spec, shifts, kernels.reshape(16, 128), *map(jnp.asarray, tables()))))
    shape = jax.ShapeDtypeStruct((8, 128, 128), F32)
    plain, lensed = pl.pallas_call(
        lens_kernel,
        out_shape=(shape, shape),
        in_specs=[hbm, hbm, vmem, vmem],
        out_specs=(hbm, hbm),
        scratch_shapes=[
            pltpu.SMEM((2, 8), jnp.int32),
            pltpu.SMEM((2, 8), jnp.int32),
            pltpu.VMEM((8, 128, 128), F32),
            dma((3,)),
            dma((8,)),
        ],
        compiler_params=pltpu.CompilerParams(vmem_limit_bytes=32 * 1024 * 1024),
    )(*(pltpu.with_memory_space_constraint(x, pltpu.HBM) for x in (sources, shifts)), ext, toep)

    def maps(x):
        return x.reshape(8, 64, 2, 128).transpose(0, 2, 1, 3).reshape(8, 2, 8192)

    return maps(plain), maps(lensed)


def solution(mesh):
    placed = (
        P(None, "lon", None, None, None, "blk"),
        P("blk", "lon", None),
        P("blk", "lon", None),
        P("blk", "lon", None, None),
    )
    return jax.shard_map(
        shards,
        mesh=mesh,
        in_specs=placed,
        out_specs=(P("blk", None, "lon"), P("blk", None, "lon")),
        check_vma=False,
    )
```

```python
import functools
import math

import jax
import jax.numpy as jnp
import numpy as np
from jax import lax
from jax.experimental import pallas as pl
from jax.experimental.pallas import tpu as pltpu
from jax.sharding import PartitionSpec as P

NBLK = 64
NLON = 4
MESH = pl.DeviceIdType.MESH
F32 = jnp.float32
BF16 = jnp.bfloat16

ROWS = 72


def tables():
    def angle(rows, cols, period):
        return 2.0 * math.pi * ((rows[:, None] * cols[None, :]) % period) / period

    i = np.arange(128)
    b = np.arange(NBLK)
    n = np.arange(256)
    first = angle(i, b, 128)
    first = np.block([[np.cos(first), -np.sin(first)], [np.sin(first), np.cos(first)]])
    turn = angle(i, n, 32768)
    pixel_rows = np.concatenate([(64 * l + np.arange(ROWS) - 4) % 256 for l in range(NLON)])
    last = angle(pixel_rows, n, 256)
    last = np.concatenate([np.cos(last), -np.sin(last)], axis=1)
    return tuple(t.astype(np.float32) for t in (first, np.cos(turn), np.sin(turn), last))


def halves(x):
    high = x.astype(BF16)
    return high, (x - high.astype(F32)).astype(BF16)


def nt(a, b):
    return lax.dot_general(a, b, (((1,), (1,)), ((), ())), preferred_element_type=F32)


def synthesize(k, land, first_ref, cos_ref, sin_ref, high_ref, low_ref, made):
    for q in range(2):
        parts = []
        for ri in range(2):
            rows = [land[k, pl.ds(4 * q + 2 * h + ri, NBLK, stride=8), :] for h in range(2)]
            parts.append(jnp.concatenate(rows, axis=1))
        xh, xl = halves(jnp.concatenate(parts, axis=0))
        spread = jnp.concatenate([xh, xh, xl], axis=0)
        g = jnp.dot(first_ref[...], spread, preferred_element_type=F32)
        gre, gim = g[:128], g[128:]
        cos, sin = cos_ref[...], sin_ref[...]
        hh, hl = halves(jnp.concatenate([gre * cos - gim * sin, gre * sin + gim * cos], axis=1))
        out = nt(high_ref[...], hh) + (nt(low_ref[...], hh) + nt(high_ref[...], hl))
        for l in range(NLON):
            made[k, l, pl.ds(q, ROWS, stride=2), :] = out[ROWS * l : ROWS * (l + 1)]


def base_of(shift):
    start = shift + 448
    base = jnp.clip(lax.shift_right_arithmetic(start, 7), 0, 6)
    return base, start - 128 * base


def place_taps(shift_ref, taps_ref, toep):
    q_index = lax.broadcasted_iota(jnp.int32, (128, 128), 0)
    u_index = lax.broadcasted_iota(jnp.int32, (128, 128), 1)
    lead = u_index - q_index

    def one(g, carry):
        for k in range(2):
            _, off = base_of(shift_ref[k, g])
            taps = jnp.broadcast_to(taps_ref[pl.ds(2 * g + k, 1), :], (8, 128))
            taps = pltpu.roll(taps, off & 127, 1)
            ring = pltpu.roll(
                jnp.broadcast_to(taps[:1], (128, 128)), 0, 1, stride=1, stride_axis=0
            )
            high = ring.astype(BF16).astype(F32)
            low = ring - high
            for i in range(3):
                at = lead + (128 * i - off)
                keep = (at >= 0) & (at < 128)
                toep[2 * g + k, :, 128 * i : 128 * i + 128] = jnp.where(keep, high, 0.0).astype(BF16)
                toep[2 * g + k, :, 128 * i + 384 : 128 * i + 512] = jnp.where(
                    keep, low, 0.0
                ).astype(BF16)
        return carry

    lax.fori_loop(0, 8, one, 0)


def lens(k, tiles, blk, src_ref, shift_ref, ext, toep, lensed_ref):
    for g in tiles:
        total = None
        for j in range(2):
            which = jnp.clip(src_ref[j, g] - blk + 1, 0, 2)
            base, _ = base_of(shift_ref[j, g])
            wins = []
            for i in range(3):
                row = 2 * (8 * g + base + i)
                wins.append(
                    jnp.concatenate(
                        [ext[k][which, l, pl.ds(row, 16), :] for l in range(NLON)], axis=0
                    )
                )
            wh, wl = halves(jnp.concatenate(wins, axis=1))
            th, tl = toep[2 * g + j, :, :384], toep[2 * g + j, :, 384:]
            part = nt(wh, th) + (nt(wl, th) + nt(wh, tl))
            total = part if total is None else total + part
        for l in range(NLON):
            lensed_ref[l, k, 16 * g : 16 * g + 16, :] = total[16 * l : 16 * l + 16]


def kernel(
    spec_ref, src_hbm, shift_hbm, taps_hbm, first_hbm, cos_hbm, sin_hbm, last_hbm,
    ext_0, ext_1, lensed_ref,
    land, made, toep, src_ref, shift_ref, taps_ref, first_ref, cos_ref, sin_ref, last_ref,
    first_cat, high_ref, low_ref,
    own_sem, send_a, recv_a, send_b, recv_b, send_c, recv_c,
):
    ext = (ext_0, ext_1)
    blk = lax.axis_index("blk")
    lon = lax.axis_index("lon")
    up = lax.rem(blk + 1, NBLK)
    down = lax.rem(blk + NBLK - 1, NBLK)

    barrier = pltpu.get_barrier_semaphore()

    def greet(o, carry):
        pl.semaphore_signal(
            barrier, inc=1, device_id=(lax.rem(blk + o, NBLK), lon), device_id_type=MESH
        )
        return carry

    lax.fori_loop(1, NBLK, greet, 0)
    for d in range(1, NLON):
        pl.semaphore_signal(
            barrier, inc=1, device_id=(blk, lax.rem(lon + d, NLON)), device_id_type=MESH
        )
    mine = pl.ds(pl.multiple_of(8 * blk, 8), 8)
    loads = [
        pltpu.make_async_copy(source, target, own_sem.at[j])
        for j, (source, target) in enumerate(
            (
                (spec_ref.at[blk, 0], land.at[0, mine]),
                (spec_ref.at[blk, 1], land.at[1, mine]),
                (src_hbm, src_ref),
                (shift_hbm, shift_ref),
                (taps_hbm, taps_ref),
                (first_hbm, first_ref),
                (cos_hbm, cos_ref),
                (sin_hbm, sin_ref),
                (last_hbm, last_ref),
            )
        )
    ]
    for load in loads:
        load.start()
    pl.semaphore_wait(barrier, NBLK - 1 + NLON - 1)

    for k in range(2):

        def send(o, carry, k=k):
            to = lax.rem(blk + o, NBLK)
            pltpu.make_async_remote_copy(
                src_ref=spec_ref.at[to, k],
                dst_ref=land.at[k, mine],
                send_sem=send_a.at[k],
                recv_sem=recv_a.at[k],
                device_id=(to, lon),
                device_id_type=MESH,
            ).start()
            return carry

        lax.fori_loop(1, NBLK, send, 0)

    for load in loads:
        load.wait()
    place_taps(shift_ref, taps_ref, toep)
    fh, fl = halves(first_ref[...])
    first_cat[...] = jnp.concatenate([fh, fl, fh], axis=1)
    lh, ll = halves(last_ref[...])
    high_ref[...] = lh
    low_ref[...] = ll

    others = [land.at[k, pl.ds(0, 8 * (NBLK - 1))] for k in range(2)]

    def across(k, d):
        to = lax.rem(lon + d, NLON)
        return pltpu.make_async_remote_copy(
            src_ref=made.at[k, to],
            dst_ref=ext[k].at[1, lon],
            send_sem=send_b.at[k, d],
            recv_sem=recv_b.at[k, d],
            device_id=(blk, to),
            device_id_type=MESH,
        )

    def beside(k, d, source, to, slot, side):
        l = lax.rem(lon + NLON - d, NLON)
        return pltpu.make_async_remote_copy(
            src_ref=source,
            dst_ref=ext[k].at[slot, l],
            send_sem=send_c.at[k, side, d],
            recv_sem=recv_c.at[k, side, d],
            device_id=(to, lon),
            device_id_type=MESH,
        )

    sent = []
    landed = [[], []]
    kept = []

    def forward(k, d):
        if d == 0:
            source = made.at[k, lon]
            keep = pltpu.make_async_copy(source, ext[k].at[1, lon], own_sem.at[9 + k])
            keep.start()
            kept.append(keep)
        else:
            across(k, d).wait_recv()
            source = ext[k].at[1, lax.rem(lon + NLON - d, NLON)]
        for to, slot, side in ((up, 0, 0), (down, 2, 1)):
            copy = beside(k, d, source, to, slot, side)
            copy.start()
            sent.append(copy)
            landed[k].append(copy)

    def turn(k):
        pltpu.make_async_copy(others[k], others[k], recv_a.at[k]).wait()
        synthesize(k, land, first_cat, cos_ref, sin_ref, high_ref, low_ref, made)
        for d in (2, 1, 3):
            copy = across(k, d)
            copy.start()
            sent.append(copy)
        forward(k, 0)

    turn(0)
    for d in (1, 3, 2):
        forward(0, d)
    turn(1)
    kept[0].wait()
    for copy in landed[0]:
        copy.wait_recv()
    first_part = functools.partial(
        lens, 0, blk=blk, src_ref=src_ref, shift_ref=shift_ref, ext=ext, toep=toep,
        lensed_ref=lensed_ref,
    )
    first_part(tiles=range(0, 3))
    forward(1, 1)
    first_part(tiles=range(3, 6))
    forward(1, 3)
    first_part(tiles=range(6, 8))
    forward(1, 2)
    kept[1].wait()
    for copy in landed[1]:
        copy.wait_recv()
    lens(1, range(8), blk, src_ref, shift_ref, ext, toep, lensed_ref)
    for k in range(2):
        pltpu.make_async_copy(others[k], others[k], send_a.at[k]).wait()
    for copy in sent:
        copy.wait_send()


def finish(ext_0, ext_1, lensed_vmem, plain_ref, lensed_ref, sems):
    copies = [
        pltpu.make_async_copy(ext_0.at[1, :, pl.ds(8, 128), :], plain_ref.at[:, 0], sems.at[0]),
        pltpu.make_async_copy(ext_1.at[1, :, pl.ds(8, 128), :], plain_ref.at[:, 1], sems.at[1]),
        pltpu.make_async_copy(lensed_vmem, lensed_ref, sems.at[2]),
    ]
    for copy in copies:
        copy.start()
    for copy in copies:
        copy.wait()


def shards(spectra, source_tiles, tap_shift, kernels):
    spec = spectra.reshape(NBLK, 2, 2, 2, 2, 128).transpose(0, 1, 2, 4, 3, 5).reshape(NBLK, 2, 8, 128)
    operands = (
        spec,
        source_tiles.transpose(0, 2, 1).reshape(2, 8),
        tap_shift.transpose(0, 2, 1).reshape(2, 8),
        kernels.reshape(16, 128),
        *map(jnp.asarray, tables()),
    )
    vmem = pl.BlockSpec(memory_space=pltpu.VMEM)
    hbm = pl.BlockSpec(memory_space=pltpu.HBM)
    dma = pltpu.SemaphoreType.DMA
    shape = jax.ShapeDtypeStruct((NLON, 2, 128, 128), F32)
    ext_0, ext_1, lensed = pl.pallas_call(
        kernel,
        out_shape=(*[jax.ShapeDtypeStruct((3, NLON, 2 * ROWS, 128), F32)] * 2, shape),
        in_specs=[hbm] * 8,
        out_specs=(vmem,) * 3,
        scratch_shapes=[
            pltpu.VMEM((2, 8 * NBLK, 128), F32),
            pltpu.VMEM((2, NLON, 2 * ROWS, 128), F32),
            pltpu.VMEM((16, 128, 768), BF16),
            pltpu.SMEM((2, 8), jnp.int32),
            pltpu.SMEM((2, 8), jnp.int32),
            pltpu.VMEM((16, 128), F32),
            pltpu.VMEM((256, 128), F32),
            pltpu.VMEM((128, 256), F32),
            pltpu.VMEM((128, 256), F32),
            pltpu.VMEM((NLON * ROWS, 512), F32),
            pltpu.VMEM((256, 384), BF16),
            pltpu.VMEM((NLON * ROWS, 512), BF16),
            pltpu.VMEM((NLON * ROWS, 512), BF16),
            dma((11,)),
            dma((2,)),
            dma((2,)),
            dma((2, NLON)),
            dma((2, NLON)),
            dma((2, 2, NLON)),
            dma((2, 2, NLON)),
        ],
        compiler_params=pltpu.CompilerParams(
            collective_id=0, has_side_effects=True, vmem_limit_bytes=32 * 1024 * 1024
        ),
    )(*(pltpu.with_memory_space_constraint(x, pltpu.HBM) for x in operands))
    plain, lensed = pl.pallas_call(
        finish,
        out_shape=(shape, shape),
        in_specs=[vmem] * 3,
        out_specs=(hbm, hbm),
        scratch_shapes=[dma((3,))],
        compiler_params=pltpu.CompilerParams(vmem_limit_bytes=16 * 1024 * 1024),
    )(ext_0, ext_1, lensed)

    def maps(x):
        return x.reshape(8, 64, 2, 128).transpose(0, 2, 1, 3).reshape(8, 2, 8192)

    return maps(plain), maps(lensed)


def solution(mesh):
    placed = (
        P(None, "lon", None, None, None, "blk"),
        P("blk", "lon", None),
        P("blk", "lon", None),
        P("blk", "lon", None, None),
    )
    return jax.shard_map(
        shards,
        mesh=mesh,
        in_specs=placed,
        out_specs=(P("blk", None, "lon"), P("blk", None, "lon")),
        check_vma=False,
    )
```

```python
import math

import jax
import jax.numpy as jnp
import numpy as np
from jax import lax
from jax.experimental import pallas as pl
from jax.experimental.pallas import tpu as pltpu
from jax.sharding import PartitionSpec as P

NBLK = 64
NLON = 4
PARTS = 4
MESH = pl.DeviceIdType.MESH
F32 = jnp.float32
BF16 = jnp.bfloat16

ROWS = 72


def tables():
    def angle(rows, cols, period):
        return 2.0 * math.pi * ((rows[:, None] * cols[None, :]) % period) / period

    i = np.arange(128)
    b = np.arange(NBLK)
    n = np.arange(256)
    turn = angle(i, b, 128)
    first = np.zeros((2, 2, 128, NBLK, 2, 2))
    for h in range(2):
        first[h, 0, :, :, h, 0] = np.cos(turn)
        first[h, 0, :, :, h, 1] = -np.sin(turn)
        first[h, 1, :, :, h, 0] = np.sin(turn)
        first[h, 1, :, :, h, 1] = np.cos(turn)
    first = first.reshape(512, 256)
    turn = angle(i, n, 32768)
    pixel_rows = np.concatenate([(64 * l + np.arange(ROWS) - 4) % 256 for l in range(NLON)])
    last = angle(pixel_rows, n, 256)
    last = np.concatenate([np.cos(last), -np.sin(last)], axis=1)
    return tuple(t.astype(np.float32) for t in (first, np.cos(turn), np.sin(turn), last))


def halves(x):
    high = x.astype(BF16)
    return high, (x - high.astype(F32)).astype(BF16)


def dot(a, b):
    return jnp.dot(a, b, preferred_element_type=F32)


def nt(a, b):
    return lax.dot_general(a, b, (((1,), (1,)), ((), ())), preferred_element_type=F32)


def synthesize(p, land, first_ref, cos_ref, sin_ref, high_ref, low_ref, made):
    xh, xl = halves(land[p].reshape(4 * NBLK, 128))
    g = dot(first_ref[...], jnp.concatenate([xh, xh, xl], axis=0))
    real, imag = [], []
    for h in range(2):
        gre, gim = g[256 * h : 256 * h + 128], g[256 * h + 128 : 256 * h + 256]
        cos, sin = cos_ref[:, 128 * h : 128 * h + 128], sin_ref[:, 128 * h : 128 * h + 128]
        real.append(gre * cos - gim * sin)
        imag.append(gre * sin + gim * cos)
    hh, hl = halves(jnp.concatenate(real + imag, axis=1))
    out = nt(high_ref[...], hh) + (nt(low_ref[...], hh) + nt(high_ref[...], hl))
    made[p] = out.reshape(NLON, ROWS, 128)


def base_of(shift):
    start = shift + 448
    base = jnp.clip(lax.shift_right_arithmetic(start, 7), 0, 6)
    return base, start - 128 * base


def place_taps(shift_ref, taps_ref, toep):
    lane = lax.broadcasted_iota(jnp.int32, (128, 128), 1)
    row = lax.broadcasted_iota(jnp.int32, (128, 128), 0)
    lead = row - lane
    flip = jnp.where(row + lane == 127, 1.0, 0.0).astype(BF16)
    high, low = halves(taps_ref[:16])
    taps_ref[...] = jnp.concatenate([dot(high, flip), dot(low, flip)], axis=0)

    def one(g, carry):
        for j in range(2):
            _, off = base_of(shift_ref[j, g])
            for half in range(2):
                taps = taps_ref[pl.ds(16 * half + 2 * g + j, 1), :]
                taps = pltpu.roll(jnp.broadcast_to(taps, (8, 128)), (129 - off) & 127, 1)
                ring = pltpu.roll(
                    jnp.broadcast_to(taps[:1], (128, 128)), 0, 1, stride=1, stride_axis=0
                )
                for i in range(3):
                    at = lead + (128 * i - off)
                    rows = slice(384 * j + 128 * i, 384 * j + 128 * i + 128)
                    toep[g, rows, 128 * half : 128 * half + 128] = jnp.where(
                        (at >= 0) & (at < 128), ring, 0.0
                    ).astype(BF16)
        return carry

    lax.fori_loop(0, 8, one, 0)


def lens(p, blk, src_ref, shift_ref, ext, toep, lensed_ref):
    for g in range(8):
        wins = []
        for j in range(2):
            which = jnp.clip(src_ref[j, g] - blk + 1, 0, 2)
            base, _ = base_of(shift_ref[j, g])
            for i in range(3):
                rows = pl.ds(8 * g + base + i, 8)
                wins.append(
                    jnp.concatenate([ext[which, l, rows, :] for l in range(NLON)], axis=0)
                )
        high, low = halves(jnp.concatenate(wins, axis=1))
        r = dot(jnp.concatenate([high, low], axis=0), toep[g])
        r = r[:, :128] + r[:, 128:]
        r = r[: 8 * NLON] + r[8 * NLON :]
        for l in range(NLON):
            lensed_ref[l, p // 2, pl.ds(16 * g + p % 2, 8, stride=2), :] = r[8 * l : 8 * l + 8]


def kernel(
    spec_ref, src_hbm, shift_hbm, taps_hbm, first_hbm, cos_hbm, sin_hbm, last_hbm,
    plain_ref, lensed_ref,
    ext_0, ext_1, ext_2, ext_3, land, made, toep, src_ref, shift_ref, taps_ref,
    first_ref, cos_ref, sin_ref, last_ref, first_cat, high_ref, low_ref,
    own_sem, send_a, recv_a, send_b, recv_b, send_c, recv_c,
):
    ext = (ext_0, ext_1, ext_2, ext_3)
    blk = lax.axis_index("blk")
    lon = lax.axis_index("lon")
    up = lax.rem(blk + 1, NBLK)
    down = lax.rem(blk + NBLK - 1, NBLK)

    barrier = pltpu.get_barrier_semaphore()

    def greet(o, carry):
        pl.semaphore_signal(
            barrier, inc=1, device_id=(lax.rem(blk + o, NBLK), lon), device_id_type=MESH
        )
        return carry

    lax.fori_loop(1, NBLK, greet, 0)
    for d in range(1, NLON):
        pl.semaphore_signal(
            barrier, inc=1, device_id=(blk, lax.rem(lon + d, NLON)), device_id_type=MESH
        )
    loads = [
        pltpu.make_async_copy(source, target, own_sem.at[j])
        for j, (source, target) in enumerate(
            [(spec_ref.at[blk, p], land.at[p, blk]) for p in range(PARTS)]
            + [
                (src_hbm, src_ref),
                (shift_hbm, shift_ref),
                (taps_hbm, taps_ref.at[pl.ds(0, 16)]),
                (first_hbm, first_ref),
                (cos_hbm, cos_ref),
                (sin_hbm, sin_ref),
                (last_hbm, last_ref),
            ]
        )
    ]
    for load in loads:
        load.start()
    pl.semaphore_wait(barrier, NBLK - 1 + NLON - 1)

    for p in range(PARTS):

        def send(o, carry, p=p):
            to = lax.rem(blk + o, NBLK)
            pltpu.make_async_remote_copy(
                src_ref=spec_ref.at[to, p],
                dst_ref=land.at[p, blk],
                send_sem=send_a.at[p],
                recv_sem=recv_a.at[p],
                device_id=(to, lon),
                device_id_type=MESH,
            ).start()
            return carry

        lax.fori_loop(1, NBLK, send, 0)

    for load in loads:
        load.wait()
    fh, fl = halves(first_ref[...])
    first_cat[...] = jnp.concatenate([fh, fl, fh], axis=1)
    lh, ll = halves(last_ref[...])
    high_ref[...] = lh
    low_ref[...] = ll
    place_taps(shift_ref, taps_ref, toep)

    others = [land.at[p, pl.ds(0, NBLK - 1)] for p in range(PARTS)]

    def across(p, d):
        to = lax.rem(lon + d, NLON)
        return pltpu.make_async_remote_copy(
            src_ref=made.at[p, to],
            dst_ref=ext[p].at[1, lon],
            send_sem=send_b.at[p, d],
            recv_sem=recv_b.at[p, d],
            device_id=(blk, to),
            device_id_type=MESH,
        )

    def beside(p, d, source, to, slot, side):
        l = lax.rem(lon + NLON - d, NLON)
        return pltpu.make_async_remote_copy(
            src_ref=source,
            dst_ref=ext[p].at[slot, l],
            send_sem=send_c.at[p, side, d],
            recv_sem=recv_c.at[p, side, d],
            device_id=(to, lon),
            device_id_type=MESH,
        )

    sent = []
    landed = [[] for _ in range(PARTS)]

    def forward(p, d):
        if d == 0:
            source = made.at[p, lon]
            keep = pltpu.make_async_copy(source, ext[p].at[1, lon], own_sem.at[11 + p])
            keep.start()
            landed[p].append(keep.wait)
        else:
            across(p, d).wait_recv()
            source = ext[p].at[1, lax.rem(lon + NLON - d, NLON)]
        for to, slot, side in ((up, 0, 0), (down, 2, 1)):
            copy = beside(p, d, source, to, slot, side)
            copy.start()
            sent.append(copy)
            landed[p].append(copy.wait_recv)

    def turn(p):
        pltpu.make_async_copy(others[p], others[p], recv_a.at[p]).wait()
        synthesize(p, land, first_cat, cos_ref, sin_ref, high_ref, low_ref, made)
        for d in (2, 1, 3):
            copy = across(p, d)
            copy.start()
            sent.append(copy)
        forward(p, 0)

    def pass_on(p):
        for d in (1, 3, 2):
            forward(p, d)

    def finish_part(p):
        for wait in landed[p]:
            wait()
        for l in range(NLON):
            plain_ref[l, p // 2, pl.ds(p % 2, 64, stride=2), :] = ext[p][1, l, 4:68, :]
        lens(p, blk, src_ref, shift_ref, ext[p], toep, lensed_ref)

    turn(0)
    turn(1)
    pass_on(0)
    turn(2)
    pass_on(1)
    finish_part(0)
    turn(3)
    pass_on(2)
    finish_part(1)
    pass_on(3)
    finish_part(2)
    finish_part(3)
    for p in range(PARTS):
        pltpu.make_async_copy(others[p], others[p], send_a.at[p]).wait()
    for copy in sent:
        copy.wait_send()


def finish(plain_vmem, lensed_vmem, plain_ref, lensed_ref, sems):
    copies = [
        pltpu.make_async_copy(plain_vmem, plain_ref, sems.at[0]),
        pltpu.make_async_copy(lensed_vmem, lensed_ref, sems.at[1]),
    ]
    for copy in copies:
        copy.start()
    for copy in copies:
        copy.wait()


def shards(spectra, source_tiles, tap_shift, kernels):
    spec = spectra.reshape(NBLK, 2, 2, 2, 2, 128).transpose(0, 1, 2, 4, 3, 5)
    operands = (
        spec.reshape(NBLK, PARTS, 4, 128),
        source_tiles.transpose(0, 2, 1).reshape(2, 8),
        tap_shift.transpose(0, 2, 1).reshape(2, 8),
        kernels.reshape(16, 128),
        *map(jnp.asarray, tables()),
    )
    vmem = pl.BlockSpec(memory_space=pltpu.VMEM)
    hbm = pl.BlockSpec(memory_space=pltpu.HBM)
    dma = pltpu.SemaphoreType.DMA
    shape = jax.ShapeDtypeStruct((NLON, 2, 128, 128), F32)
    maps_in_vmem = pl.pallas_call(
        kernel,
        out_shape=(shape, shape),
        in_specs=[hbm] * 8,
        out_specs=(vmem, vmem),
        scratch_shapes=[pltpu.VMEM((3, NLON, ROWS, 128), F32)] * PARTS
        + [
            pltpu.VMEM((PARTS, NBLK, 4, 128), F32),
            pltpu.VMEM((PARTS, NLON, ROWS, 128), F32),
            pltpu.VMEM((8, 768, 256), BF16),
            pltpu.SMEM((2, 8), jnp.int32),
            pltpu.SMEM((2, 8), jnp.int32),
            pltpu.VMEM((32, 128), F32),
            pltpu.VMEM((512, 256), F32),
            pltpu.VMEM((128, 256), F32),
            pltpu.VMEM((128, 256), F32),
            pltpu.VMEM((NLON * ROWS, 512), F32),
            pltpu.VMEM((512, 768), BF16),
            pltpu.VMEM((NLON * ROWS, 512), BF16),
            pltpu.VMEM((NLON * ROWS, 512), BF16),
            dma((11 + PARTS,)),
            dma((PARTS,)),
            dma((PARTS,)),
            dma((PARTS, NLON)),
            dma((PARTS, NLON)),
            dma((PARTS, 2, NLON)),
            dma((PARTS, 2, NLON)),
        ],
        compiler_params=pltpu.CompilerParams(
            collective_id=0, has_side_effects=True, vmem_limit_bytes=32 * 1024 * 1024
        ),
    )(*(pltpu.with_memory_space_constraint(x, pltpu.HBM) for x in operands))
    plain, lensed = pl.pallas_call(
        finish,
        out_shape=(shape, shape),
        in_specs=[vmem, vmem],
        out_specs=(hbm, hbm),
        scratch_shapes=[dma((2,))],
        compiler_params=pltpu.CompilerParams(vmem_limit_bytes=16 * 1024 * 1024),
    )(*maps_in_vmem)

    def maps(x):
        return x.reshape(8, 64, 2, 128).transpose(0, 2, 1, 3).reshape(8, 2, 8192)

    return maps(plain), maps(lensed)


def solution(mesh):
    placed = (
        P(None, "lon", None, None, None, "blk"),
        P("blk", "lon", None),
        P("blk", "lon", None),
        P("blk", "lon", None, None),
    )
    return jax.shard_map(
        shards,
        mesh=mesh,
        in_specs=placed,
        out_specs=(P("blk", None, "lon"), P("blk", None, "lon")),
        check_vma=False,
    )
```

```python
import math

import jax
import jax.numpy as jnp
import numpy as np
from jax import lax
from jax.experimental import pallas as pl
from jax.experimental.pallas import tpu as pltpu
from jax.sharding import PartitionSpec as P

NBLK = 64
NLON = 4
PARTS = 4
MESH = pl.DeviceIdType.MESH
F32 = jnp.float32
BF16 = jnp.bfloat16

ROWS = 72


def tables():
    def angle(rows, cols, period):
        return 2.0 * math.pi * ((rows[:, None] * cols[None, :]) % period) / period

    i = np.arange(128)
    b = np.arange(NBLK)
    n = np.arange(256)
    turn = angle(i, b, 128)
    first = np.zeros((2, 2, 128, NBLK, 2, 2))
    for h in range(2):
        first[h, 0, :, :, h, 0] = np.cos(turn)
        first[h, 0, :, :, h, 1] = -np.sin(turn)
        first[h, 1, :, :, h, 0] = np.sin(turn)
        first[h, 1, :, :, h, 1] = np.cos(turn)
    first = first.reshape(512, 256)
    turn = angle(i, n, 32768)
    pixel_rows = np.concatenate([(64 * l + np.arange(ROWS) - 4) % 256 for l in range(NLON)])
    last = angle(pixel_rows, n, 256)
    last = np.concatenate([np.cos(last), -np.sin(last)], axis=1)
    return tuple(t.astype(np.float32) for t in (first, np.cos(turn), np.sin(turn), last))


def halves(x):
    high = x.astype(BF16)
    return high, (x - high.astype(F32)).astype(BF16)


def dot(a, b):
    return jnp.dot(a, b, preferred_element_type=F32)


def nt(a, b):
    return lax.dot_general(a, b, (((1,), (1,)), ((), ())), preferred_element_type=F32)


def synthesize(p, land, first_ref, cos_ref, sin_ref, last_ref, made):
    x = jnp.concatenate(halves(land[p].reshape(4 * NBLK, 128)), axis=1)
    r = dot(first_ref[...], x)
    g = r[:512, :128] + (r[:512, 128:] + r[512:, :128])
    real, imag = [], []
    for h in range(2):
        gre, gim = g[256 * h : 256 * h + 128], g[256 * h + 128 : 256 * h + 256]
        cos, sin = cos_ref[:, 128 * h : 128 * h + 128], sin_ref[:, 128 * h : 128 * h + 128]
        real.append(gre * cos - gim * sin)
        imag.append(gre * sin + gim * cos)
    r = nt(last_ref[...], jnp.concatenate(halves(jnp.concatenate(real + imag, axis=1)), axis=0))
    count = NLON * ROWS
    made[p] = (r[:count, :128] + (r[:count, 128:] + r[count:, :128])).reshape(NLON, ROWS, 128)


def base_of(shift):
    start = shift + 448
    base = jnp.clip(lax.shift_right_arithmetic(start, 7), 0, 6)
    return base, start - 128 * base


def place_taps(shift_ref, taps_ref, toep):
    lane = lax.broadcasted_iota(jnp.int32, (128, 128), 1)
    row = lax.broadcasted_iota(jnp.int32, (128, 128), 0)
    lead = row - lane
    flip = jnp.where(row + lane == 127, 1.0, 0.0).astype(BF16)
    high, low = halves(taps_ref[:16])
    taps_ref[...] = jnp.concatenate([dot(high, flip), dot(low, flip)], axis=0)

    def one(g, carry):
        for j in range(2):
            _, off = base_of(shift_ref[j, g])
            for half in range(2):
                taps = taps_ref[pl.ds(16 * half + 2 * g + j, 1), :]
                taps = pltpu.roll(jnp.broadcast_to(taps, (8, 128)), (129 - off) & 127, 1)
                ring = pltpu.roll(
                    jnp.broadcast_to(taps[:1], (128, 128)), 0, 1, stride=1, stride_axis=0
                )
                for i in range(3):
                    at = lead + (128 * i - off)
                    rows = slice(384 * j + 128 * i, 384 * j + 128 * i + 128)
                    toep[g, rows, 128 * half : 128 * half + 128] = jnp.where(
                        (at >= 0) & (at < 128), ring, 0.0
                    ).astype(BF16)
        return carry

    lax.fori_loop(0, 8, one, 0)


def lens(p, blk, src_ref, shift_ref, ext, toep, lensed_ref):
    for g in range(8):
        wins = []
        for j in range(2):
            which = jnp.clip(src_ref[j, g] - blk + 1, 0, 2)
            base, _ = base_of(shift_ref[j, g])
            for i in range(3):
                rows = pl.ds(8 * g + base + i, 8)
                wins.append(
                    jnp.concatenate([ext[which, l, rows, :] for l in range(NLON)], axis=0)
                )
        high, low = halves(jnp.concatenate(wins, axis=1))
        r = dot(jnp.concatenate([high, low], axis=0), toep[g])
        r = r[:, :128] + r[:, 128:]
        r = r[: 8 * NLON] + r[8 * NLON :]
        for l in range(NLON):
            lensed_ref[l, p // 2, pl.ds(16 * g + p % 2, 8, stride=2), :] = r[8 * l : 8 * l + 8]


def kernel(
    spec_ref, src_hbm, shift_hbm, taps_hbm, first_hbm, cos_hbm, sin_hbm, last_hbm,
    plain_ref, lensed_ref,
    ext_0, ext_1, ext_2, ext_3, land, made, toep, src_ref, shift_ref, taps_ref,
    first_ref, cos_ref, sin_ref, last_ref, first_cat, last_cat,
    own_sem, send_a, recv_a, send_b, recv_b, send_c, recv_c,
):
    ext = (ext_0, ext_1, ext_2, ext_3)
    blk = lax.axis_index("blk")
    lon = lax.axis_index("lon")
    up = lax.rem(blk + 1, NBLK)
    down = lax.rem(blk + NBLK - 1, NBLK)
    odd = lax.rem(blk, 2)
    near = blk + 1 - 2 * odd
    far = lax.rem(blk + NBLK - 1 + 2 * odd, NBLK)

    barrier = pltpu.get_barrier_semaphore()

    def greet(o, carry):
        pl.semaphore_signal(
            barrier, inc=1, device_id=(lax.rem(blk + o, NBLK), lon), device_id_type=MESH
        )
        return carry

    lax.fori_loop(1, NBLK, greet, 0, unroll=9)
    for d in range(1, NLON):
        for to in (blk, far):
            pl.semaphore_signal(
                barrier, inc=1, device_id=(to, lax.rem(lon + d, NLON)), device_id_type=MESH
            )
    loads = [
        pltpu.make_async_copy(source, target, own_sem.at[j])
        for j, (source, target) in enumerate(
            [(spec_ref.at[blk, p], land.at[p, blk]) for p in range(PARTS)]
            + [
                (src_hbm, src_ref),
                (shift_hbm, shift_ref),
                (taps_hbm, taps_ref.at[pl.ds(0, 16)]),
                (first_hbm, first_ref),
                (cos_hbm, cos_ref),
                (sin_hbm, sin_ref),
                (last_hbm, last_ref),
            ]
        )
    ]
    for load in loads:
        load.start()
    pl.semaphore_wait(barrier, NBLK - 1 + 2 * (NLON - 1))

    for p in range(PARTS):

        def send(o, carry, p=p):
            to = lax.rem(blk + o, NBLK)
            pltpu.make_async_remote_copy(
                src_ref=spec_ref.at[to, p],
                dst_ref=land.at[p, blk],
                send_sem=send_a.at[p],
                recv_sem=recv_a.at[p],
                device_id=(to, lon),
                device_id_type=MESH,
            ).start()
            return carry

        lax.fori_loop(1, NBLK, send, 0, unroll=3)

    for load in loads:
        load.wait()
    first_cat[...] = jnp.concatenate(halves(first_ref[...]), axis=0)
    last_cat[...] = jnp.concatenate(halves(last_ref[...]), axis=0)
    place_taps(shift_ref, taps_ref, toep)

    others = [land.at[p, pl.ds(0, NBLK - 1)] for p in range(PARTS)]

    def across(p, d):
        to = lax.rem(lon + d, NLON)
        return pltpu.make_async_remote_copy(
            src_ref=made.at[p, to],
            dst_ref=ext[p].at[1, lon],
            send_sem=send_b,
            recv_sem=recv_b.at[p, d],
            device_id=(blk, to),
            device_id_type=MESH,
        )

    def beside(p, source, l, row, to, slot):
        pltpu.make_async_remote_copy(
            src_ref=source,
            dst_ref=ext[p].at[slot, l],
            send_sem=send_c.at[p],
            recv_sem=recv_c.at[p],
            device_id=(row, to),
            device_id_type=MESH,
        ).start()

    def keep(p):
        return pltpu.make_async_copy(made.at[p, lon], ext[p].at[1, lon], own_sem.at[11 + p])

    def pass_on(p, d):
        l = lax.rem(lon + NLON - d, NLON)
        if d == 0:
            source = made.at[p, lon]
        else:
            across(p, d).wait_recv()
            source = ext[p].at[1, l]
        if p < PARTS - 1:
            beside(p, source, l, up, lon, 0)
            beside(p, source, l, down, lon, 2)
        else:
            beside(p, source, l, near, lon, 2 * odd)

    def turn(p):
        pltpu.make_async_copy(others[p], others[p], recv_a.at[p]).wait()
        synthesize(p, land, first_cat, cos_ref, sin_ref, last_cat, made)
        for d in (2, 1, 3, 0):
            to = lax.rem(lon + d, NLON)
            if p == PARTS - 1:
                beside(p, made.at[p, to], lon, far, to, 2 - 2 * odd)
            if d != 0:
                across(p, d).start()
        pass_on(p, 0)
        keep(p).start()

    def finish_part(p):
        rows = ext[p].at[pl.ds(0, 2)]
        pltpu.make_async_copy(rows, rows, recv_c.at[p]).wait()
        keep(p).wait()
        for l in range(NLON):
            plain_ref[l, p // 2, pl.ds(p % 2, 64, stride=2), :] = ext[p][1, l, 4:68, :]
        lens(p, blk, src_ref, shift_ref, ext[p], toep, lensed_ref)

    def sent(p):
        rows = ext[p].at[pl.ds(0, 2)]
        pltpu.make_async_copy(rows, rows, send_c.at[p]).wait()
        pltpu.make_async_copy(others[p], others[p], send_a.at[p]).wait()

    turn(0)
    turn(1)
    for d in (1, 3, 2):
        pass_on(0, d)
    turn(2)
    for d in (1, 3, 2):
        pass_on(1, d)
    finish_part(0)
    turn(3)
    for d in (1, 3, 2):
        pass_on(2, d)
    finish_part(1)
    for d in (1, 3, 2):
        pass_on(3, d)
    finish_part(2)
    for p in range(3):
        sent(p)
    every = made.at[:, pl.ds(0, NLON - 1)]
    pltpu.make_async_copy(every, every, send_b).wait()
    finish_part(3)
    sent(3)


def finish(plain_vmem, lensed_vmem, plain_ref, lensed_ref, sems):
    copies = [
        pltpu.make_async_copy(source.at[l], target.at[l], sems.at[j, l])
        for j, (source, target) in enumerate(((plain_vmem, plain_ref), (lensed_vmem, lensed_ref)))
        for l in range(NLON)
    ]
    for copy in copies:
        copy.start()
    for copy in copies:
        copy.wait()


def shards(spectra, source_tiles, tap_shift, kernels):
    spec = spectra.reshape(NBLK, 2, 2, 2, 2, 128).transpose(0, 1, 2, 4, 3, 5)
    operands = (
        spec.reshape(NBLK, PARTS, 4, 128),
        source_tiles.transpose(0, 2, 1).reshape(2, 8),
        tap_shift.transpose(0, 2, 1).reshape(2, 8),
        kernels.reshape(16, 128),
        *map(jnp.asarray, tables()),
    )
    vmem = pl.BlockSpec(memory_space=pltpu.VMEM)
    hbm = pl.BlockSpec(memory_space=pltpu.HBM)
    dma = pltpu.SemaphoreType.DMA
    shape = jax.ShapeDtypeStruct((NLON, 2, 128, 128), F32)
    maps_in_vmem = pl.pallas_call(
        kernel,
        out_shape=(shape, shape),
        in_specs=[hbm] * 8,
        out_specs=(vmem, vmem),
        scratch_shapes=[pltpu.VMEM((3, NLON, ROWS, 128), F32)] * PARTS
        + [
            pltpu.VMEM((PARTS, NBLK, 4, 128), F32),
            pltpu.VMEM((PARTS, NLON, ROWS, 128), F32),
            pltpu.VMEM((8, 768, 256), BF16),
            pltpu.SMEM((2, 8), jnp.int32),
            pltpu.SMEM((2, 8), jnp.int32),
            pltpu.VMEM((32, 128), F32),
            pltpu.VMEM((512, 256), F32),
            pltpu.VMEM((128, 256), F32),
            pltpu.VMEM((128, 256), F32),
            pltpu.VMEM((NLON * ROWS, 512), F32),
            pltpu.VMEM((1024, 256), BF16),
            pltpu.VMEM((2 * NLON * ROWS, 512), BF16),
            dma((11 + PARTS,)),
            dma((PARTS,)),
            dma((PARTS,)),
            dma,
            dma((PARTS, NLON)),
            dma((PARTS,)),
            dma((PARTS,)),
        ],
        compiler_params=pltpu.CompilerParams(
            collective_id=0, has_side_effects=True, vmem_limit_bytes=32 * 1024 * 1024
        ),
    )(*(pltpu.with_memory_space_constraint(x, pltpu.HBM) for x in operands))
    plain, lensed = pl.pallas_call(
        finish,
        out_shape=(shape, shape),
        in_specs=[vmem, vmem],
        out_specs=(hbm, hbm),
        scratch_shapes=[dma((2, NLON))],
        compiler_params=pltpu.CompilerParams(vmem_limit_bytes=16 * 1024 * 1024),
    )(*maps_in_vmem)

    def maps(x):
        return x.reshape(8, 64, 2, 128).transpose(0, 2, 1, 3).reshape(8, 2, 8192)

    return maps(plain), maps(lensed)


def solution(mesh):
    placed = (
        P(None, "lon", None, None, None, "blk"),
        P("blk", "lon", None),
        P("blk", "lon", None),
        P("blk", "lon", None, None),
    )
    return jax.shard_map(
        shards,
        mesh=mesh,
        in_specs=placed,
        out_specs=(P("blk", None, "lon"), P("blk", None, "lon")),
        check_vma=False,
    )
```

```python
import math

import jax
import jax.numpy as jnp
import numpy as np
from jax import lax
from jax.experimental import pallas as pl
from jax.experimental.pallas import tpu as pltpu
from jax.sharding import PartitionSpec as P

NBLK = 64
NLON = 4
PARTS = 4
DIRECT = 2
MESH = pl.DeviceIdType.MESH
F32 = jnp.float32
BF16 = jnp.bfloat16

ROWS = 72


def tables():
    def angle(rows, cols, period):
        return 2.0 * math.pi * ((rows[:, None] * cols[None, :]) % period) / period

    i = np.arange(128)
    b = np.arange(NBLK)
    n = np.arange(256)
    turn = angle(i, b, 128)
    first = np.zeros((2, 2, 128, NBLK, 2, 2))
    for h in range(2):
        first[h, 0, :, :, h, 0] = np.cos(turn)
        first[h, 0, :, :, h, 1] = -np.sin(turn)
        first[h, 1, :, :, h, 0] = np.sin(turn)
        first[h, 1, :, :, h, 1] = np.cos(turn)
    first = first.reshape(512, 256)
    turn = angle(i, n, 32768)
    pixel_rows = np.concatenate([(64 * l + np.arange(ROWS) - 4) % 256 for l in range(NLON)])
    last = angle(pixel_rows, n, 256)
    last = np.concatenate([np.cos(last), -np.sin(last)], axis=1)
    return tuple(t.astype(np.float32) for t in (first, np.cos(turn), np.sin(turn), last))


def halves(x):
    high = x.astype(BF16)
    return high, (x - high.astype(F32)).astype(BF16)


def dot(a, b):
    return jnp.dot(a, b, preferred_element_type=F32)


def nt(a, b):
    return lax.dot_general(a, b, (((1,), (1,)), ((), ())), preferred_element_type=F32)


def transform(p, land, first_ref, cos_ref, sin_ref):
    x = jnp.concatenate(halves(land[p].reshape(4 * NBLK, 128)), axis=1)
    r = dot(first_ref[...], x)
    g = r[:512, :128] + (r[:512, 128:] + r[512:, :128])
    real, imag = [], []
    for h in range(2):
        gre, gim = g[256 * h : 256 * h + 128], g[256 * h + 128 : 256 * h + 256]
        cos, sin = cos_ref[:, 128 * h : 128 * h + 128], sin_ref[:, 128 * h : 128 * h + 128]
        real.append(gre * cos - gim * sin)
        imag.append(gre * sin + gim * cos)
    return jnp.concatenate(halves(jnp.concatenate(real + imag, axis=1)), axis=0)


def pixels(last_ref, l, turned):
    r = nt(last_ref[pl.ds(pl.multiple_of(2 * ROWS * l, 16), 2 * ROWS), :], turned)
    return r[:ROWS, :128] + (r[:ROWS, 128:] + r[ROWS:, :128])


def base_of(shift):
    start = shift + 448
    base = jnp.clip(lax.shift_right_arithmetic(start, 7), 0, 6)
    return base, start - 128 * base


def place_taps(shift_ref, taps_ref, toep):
    lane = lax.broadcasted_iota(jnp.int32, (128, 128), 1)
    row = lax.broadcasted_iota(jnp.int32, (128, 128), 0)
    lead = row - lane
    flip = jnp.where(row + lane == 127, 1.0, 0.0).astype(BF16)
    high, low = halves(taps_ref[:16])
    taps_ref[...] = jnp.concatenate([dot(high, flip), dot(low, flip)], axis=0)

    def one(g, carry):
        for j in range(2):
            _, off = base_of(shift_ref[j, g])
            for half in range(2):
                taps = taps_ref[pl.ds(16 * half + 2 * g + j, 1), :]
                taps = pltpu.roll(jnp.broadcast_to(taps, (8, 128)), (129 - off) & 127, 1)
                ring = pltpu.roll(
                    jnp.broadcast_to(taps[:1], (128, 128)), 0, 1, stride=1, stride_axis=0
                )
                for i in range(3):
                    at = lead + (128 * i - off)
                    rows = slice(384 * j + 128 * i, 384 * j + 128 * i + 128)
                    toep[g, rows, 128 * half : 128 * half + 128] = jnp.where(
                        (at >= 0) & (at < 128), ring, 0.0
                    ).astype(BF16)
        return carry

    lax.fori_loop(0, 8, one, 0)


def lens(p, blk, src_ref, shift_ref, ext, toep, lensed_ref):
    for g in range(8):
        wins = []
        for j in range(2):
            which = jnp.clip(src_ref[j, g] - blk + 1, 0, 2)
            base, _ = base_of(shift_ref[j, g])
            for i in range(3):
                rows = pl.ds(8 * g + base + i, 8)
                wins.append(
                    jnp.concatenate([ext[which, l, rows, :] for l in range(NLON)], axis=0)
                )
        high, low = halves(jnp.concatenate(wins, axis=1))
        r = dot(jnp.concatenate([high, low], axis=0), toep[g])
        r = r[:, :128] + r[:, 128:]
        r = r[: 8 * NLON] + r[8 * NLON :]
        for l in range(NLON):
            lensed_ref[l, p // 2, pl.ds(16 * g + p % 2, 8, stride=2), :] = r[8 * l : 8 * l + 8]


def kernel(
    spec_ref, src_hbm, shift_hbm, taps_hbm, first_hbm, cos_hbm, sin_hbm, last_hbm,
    plain_ref, lensed_ref,
    ext_0, ext_1, ext_2, ext_3, land, made, toep, src_ref, shift_ref, taps_ref,
    first_ref, cos_ref, sin_ref, last_ref, first_cat, last_cat,
    own_sem, send_a, recv_a, send_b, recv_b, send_c, recv_c,
):
    ext = (ext_0, ext_1, ext_2, ext_3)
    blk = lax.axis_index("blk")
    lon = lax.axis_index("lon")
    odd = lax.rem(blk, 2)
    near = blk + 1 - 2 * odd
    far = blk - 1 + 2 * odd
    has_far = (blk > 0) & (blk < NBLK - 1)

    barrier = pltpu.get_barrier_semaphore()

    def greet(o, carry):
        pl.semaphore_signal(
            barrier, inc=1, device_id=(lax.rem(blk + o, NBLK), lon), device_id_type=MESH
        )
        return carry

    lax.fori_loop(1, NBLK, greet, 0, unroll=9)
    for d in range(1, NLON):
        pl.semaphore_signal(
            barrier, inc=1, device_id=(blk, lax.rem(lon + d, NLON)), device_id_type=MESH
        )

    @pl.when(has_far)
    def _():
        for d in range(1, NLON):
            pl.semaphore_signal(
                barrier, inc=1, device_id=(far, lax.rem(lon + d, NLON)), device_id_type=MESH
            )

    loads = [
        pltpu.make_async_copy(source, target, own_sem.at[j])
        for j, (source, target) in enumerate(
            [(spec_ref.at[blk, p], land.at[p, blk]) for p in range(PARTS)]
            + [
                (src_hbm, src_ref),
                (shift_hbm, shift_ref),
                (taps_hbm, taps_ref.at[pl.ds(0, 16)]),
                (first_hbm, first_ref),
                (cos_hbm, cos_ref),
                (sin_hbm, sin_ref),
                (last_hbm, last_ref),
            ]
        )
    ]
    for load in loads:
        load.start()
    pl.semaphore_wait(
        barrier, NBLK - 1 + (NLON - 1) * (1 + has_far.astype(jnp.int32))
    )

    for p in range(PARTS):

        def send(o, carry, p=p):
            to = 8 * (o // 8) + lax.rem(blk + o, 8)

            @pl.when(to != blk)
            def _():
                pltpu.make_async_remote_copy(
                    src_ref=spec_ref.at[to, p],
                    dst_ref=land.at[p, blk],
                    send_sem=send_a.at[p],
                    recv_sem=recv_a.at[p],
                    device_id=(to, lon),
                    device_id_type=MESH,
                ).start()

            return carry

        lax.fori_loop(0, NBLK, send, 0)

    for load in loads:
        load.wait()
    first_cat[...] = jnp.concatenate(halves(first_ref[...]), axis=0)
    for l in range(NLON):
        last_cat[2 * ROWS * l : 2 * ROWS * (l + 1)] = jnp.concatenate(
            halves(last_ref[ROWS * l : ROWS * (l + 1)]), axis=0
        )
    place_taps(shift_ref, taps_ref, toep)

    others = [land.at[p, pl.ds(0, NBLK - 1)] for p in range(PARTS)]

    def across(p, d):
        to = lax.rem(lon + d, NLON)
        return pltpu.make_async_remote_copy(
            src_ref=made.at[p, to],
            dst_ref=ext[p].at[1, lon],
            send_sem=send_b,
            recv_sem=recv_b.at[p, d],
            device_id=(blk, to),
            device_id_type=MESH,
        )

    def beside(p, source, l, row, to, slot, side):
        pltpu.make_async_remote_copy(
            src_ref=source,
            dst_ref=ext[p].at[slot, l],
            send_sem=send_c.at[side, p],
            recv_sem=recv_c.at[side, p],
            device_id=(row, to),
            device_id_type=MESH,
        ).start()

    def to_near(p, source, l):
        beside(p, source, l, near, lon, 2 * odd, 0)

    def to_far(p, source, l, to):
        @pl.when(has_far)
        def _():
            beside(p, source, l, far, to, 2 - 2 * odd, 1)

    def keep(p):
        return pltpu.make_async_copy(made.at[p, lon], ext[p].at[1, lon], own_sem.at[11 + p])

    def turn(p):
        pltpu.make_async_copy(others[p], others[p], recv_a.at[p]).wait()
        turned = transform(p, land, first_cat, cos_ref, sin_ref)
        for d in (2, 1, 3, 0):
            to = lax.rem(lon + d, NLON)
            made[p, to] = pixels(last_cat, to, turned)
            if d != 0:
                across(p, d).start()
            if d == 0 or p >= DIRECT:
                to_far(p, made.at[p, to], lon, to)
        to_near(p, made.at[p, lon], lon)
        keep(p).start()

    def pass_on(p):
        for d in (1, 3, 2):
            l = lax.rem(lon + NLON - d, NLON)
            across(p, d).wait_recv()
            to_near(p, ext[p].at[1, l], l)
            if p < DIRECT:
                to_far(p, ext[p].at[1, l], l, lon)

    def finish_part(p):
        keep(p).wait()
        for l in range(NLON):
            plain_ref[l, p // 2, pl.ds(p % 2, 64, stride=2), :] = ext[p][1, l, 4:68, :]
        rows = ext[p].at[0]
        pltpu.make_async_copy(rows, rows, recv_c.at[0, p]).wait()

        @pl.when(has_far)
        def _():
            pltpu.make_async_copy(rows, rows, recv_c.at[1, p]).wait()

        lens(p, blk, src_ref, shift_ref, ext[p], toep, lensed_ref)

    def sent(p):
        rows = ext[p].at[0]
        pltpu.make_async_copy(rows, rows, send_c.at[0, p]).wait()

        @pl.when(has_far)
        def _():
            pltpu.make_async_copy(rows, rows, send_c.at[1, p]).wait()

        pltpu.make_async_copy(others[p], others[p], send_a.at[p]).wait()

    turn(0)
    turn(1)
    pass_on(0)
    turn(2)
    pass_on(1)
    finish_part(0)
    turn(3)
    pass_on(2)
    finish_part(1)
    pass_on(3)
    for p in range(3):
        sent(p)
    finish_part(2)
    every = made.at[:, pl.ds(0, NLON - 1)]
    pltpu.make_async_copy(every, every, send_b).wait()
    finish_part(3)
    sent(3)


def finish(plain_vmem, lensed_vmem, plain_ref, lensed_ref, sems):
    copies = [
        pltpu.make_async_copy(source.at[l], target.at[l], sems.at[j, l])
        for j, (source, target) in enumerate(((plain_vmem, plain_ref), (lensed_vmem, lensed_ref)))
        for l in range(NLON)
    ]
    for copy in copies:
        copy.start()
    for copy in copies:
        copy.wait()


def shards(spectra, source_tiles, tap_shift, kernels):
    spec = spectra.reshape(NBLK, 2, 2, 2, 2, 128).transpose(0, 1, 2, 4, 3, 5)
    operands = (
        spec.reshape(NBLK, PARTS, 4, 128),
        source_tiles.transpose(0, 2, 1).reshape(2, 8),
        tap_shift.transpose(0, 2, 1).reshape(2, 8),
        kernels.reshape(16, 128),
        *map(jnp.asarray, tables()),
    )
    vmem = pl.BlockSpec(memory_space=pltpu.VMEM)
    hbm = pl.BlockSpec(memory_space=pltpu.HBM)
    dma = pltpu.SemaphoreType.DMA
    shape = jax.ShapeDtypeStruct((NLON, 2, 128, 128), F32)
    maps_in_vmem = pl.pallas_call(
        kernel,
        out_shape=(shape, shape),
        in_specs=[hbm] * 8,
        out_specs=(vmem, vmem),
        scratch_shapes=[pltpu.VMEM((3, NLON, ROWS, 128), F32)] * PARTS
        + [
            pltpu.VMEM((PARTS, NBLK, 4, 128), F32),
            pltpu.VMEM((PARTS, NLON, ROWS, 128), F32),
            pltpu.VMEM((8, 768, 256), BF16),
            pltpu.SMEM((2, 8), jnp.int32),
            pltpu.SMEM((2, 8), jnp.int32),
            pltpu.VMEM((32, 128), F32),
            pltpu.VMEM((512, 256), F32),
            pltpu.VMEM((128, 256), F32),
            pltpu.VMEM((128, 256), F32),
            pltpu.VMEM((NLON * ROWS, 512), F32),
            pltpu.VMEM((1024, 256), BF16),
            pltpu.VMEM((2 * NLON * ROWS, 512), BF16),
            dma((11 + PARTS,)),
            dma((PARTS,)),
            dma((PARTS,)),
            dma,
            dma((PARTS, NLON)),
            dma((2, PARTS)),
            dma((2, PARTS)),
        ],
        compiler_params=pltpu.CompilerParams(
            collective_id=0, has_side_effects=True, vmem_limit_bytes=32 * 1024 * 1024
        ),
    )(*(pltpu.with_memory_space_constraint(x, pltpu.HBM) for x in operands))
    plain, lensed = pl.pallas_call(
        finish,
        out_shape=(shape, shape),
        in_specs=[vmem, vmem],
        out_specs=(hbm, hbm),
        scratch_shapes=[dma((2, NLON))],
        compiler_params=pltpu.CompilerParams(vmem_limit_bytes=16 * 1024 * 1024),
    )(*maps_in_vmem)

    def maps(x):
        return x.reshape(8, 64, 2, 128).transpose(0, 2, 1, 3).reshape(8, 2, 8192)

    return maps(plain), maps(lensed)


def solution(mesh):
    placed = (
        P(None, "lon", None, None, None, "blk"),
        P("blk", "lon", None),
        P("blk", "lon", None),
        P("blk", "lon", None, None),
    )
    return jax.shard_map(
        shards,
        mesh=mesh,
        in_specs=placed,
        out_specs=(P("blk", None, "lon"), P("blk", None, "lon")),
        check_vma=False,
    )
```

```python
import math

import jax
import jax.numpy as jnp
import numpy as np
from jax import lax
from jax.experimental import pallas as pl
from jax.experimental.pallas import tpu as pltpu
from jax.sharding import PartitionSpec as P

NBLK = 64
NLON = 4
PARTS = 4
DIRECT = 2
MESH = pl.DeviceIdType.MESH
F32 = jnp.float32
BF16 = jnp.bfloat16

ROWS = 72


def tables():
    def angle(rows, cols, period):
        return 2.0 * math.pi * ((rows[:, None] * cols[None, :]) % period) / period

    i = np.arange(128)
    b = np.arange(NBLK)
    n = np.arange(256)
    turn = angle(i, b, 128)
    first = np.zeros((2, 2, 128, NBLK, 2, 2))
    for h in range(2):
        first[h, 0, :, :, h, 0] = np.cos(turn)
        first[h, 0, :, :, h, 1] = -np.sin(turn)
        first[h, 1, :, :, h, 0] = np.sin(turn)
        first[h, 1, :, :, h, 1] = np.cos(turn)
    first = first.reshape(512, 256)
    turn = angle(i, n, 32768)
    pixel_rows = np.concatenate([(64 * l + np.arange(ROWS) - 4) % 256 for l in range(NLON)])
    last = angle(pixel_rows, n, 256)
    last = np.concatenate([np.cos(last), -np.sin(last)], axis=1)
    return tuple(t.astype(np.float32) for t in (first, np.cos(turn), np.sin(turn), last))


def halves(x):
    high = x.astype(BF16)
    return high, (x - high.astype(F32)).astype(BF16)


def dot(a, b):
    return jnp.dot(a, b, preferred_element_type=F32)


def nt(a, b):
    return lax.dot_general(a, b, (((1,), (1,)), ((), ())), preferred_element_type=F32)


def transform(p, land, first_ref, cos_ref, sin_ref):
    x = jnp.concatenate(halves(land[p].reshape(4 * NBLK, 128)), axis=1)
    r = dot(first_ref[...], x)
    g = r[:512, :128] + (r[:512, 128:] + r[512:, :128])
    real, imag = [], []
    for h in range(2):
        gre, gim = g[256 * h : 256 * h + 128], g[256 * h + 128 : 256 * h + 256]
        cos, sin = cos_ref[:, 128 * h : 128 * h + 128], sin_ref[:, 128 * h : 128 * h + 128]
        real.append(gre * cos - gim * sin)
        imag.append(gre * sin + gim * cos)
    return jnp.concatenate(halves(jnp.concatenate(real + imag, axis=1)), axis=0)


def pixels(last_ref, l, turned):
    r = nt(last_ref[pl.ds(pl.multiple_of(2 * ROWS * l, 16), 2 * ROWS), :], turned)
    return r[:ROWS, :128] + (r[:ROWS, 128:] + r[ROWS:, :128])


def base_of(shift):
    start = shift + 448
    base = jnp.clip(lax.shift_right_arithmetic(start, 7), 0, 6)
    return base, start - 128 * base


def place_taps(shift_ref, taps_ref, toep):
    lane = lax.broadcasted_iota(jnp.int32, (128, 128), 1)
    row = lax.broadcasted_iota(jnp.int32, (128, 128), 0)
    lead = row - lane
    flip = jnp.where(row + lane == 127, 1.0, 0.0).astype(BF16)
    high, low = halves(taps_ref[:16])
    taps_ref[...] = jnp.concatenate([dot(high, flip), dot(low, flip)], axis=0)

    def one(g, carry):
        for j in range(2):
            _, off = base_of(shift_ref[j, g])
            for half in range(2):
                taps = taps_ref[pl.ds(16 * half + 2 * g + j, 1), :]
                taps = pltpu.roll(jnp.broadcast_to(taps, (8, 128)), (129 - off) & 127, 1)
                ring = pltpu.roll(
                    jnp.broadcast_to(taps[:1], (128, 128)), 0, 1, stride=1, stride_axis=0
                )
                for i in range(3):
                    at = lead + (128 * i - off)
                    rows = slice(384 * j + 128 * i, 384 * j + 128 * i + 128)
                    toep[g, rows, 128 * half : 128 * half + 128] = jnp.where(
                        (at >= 0) & (at < 128), ring, 0.0
                    ).astype(BF16)
        return carry

    lax.fori_loop(0, 8, one, 0)


def lens(p, blk, src_ref, shift_ref, ext, toep, lensed_ref):
    for g in range(8):
        wins = []
        for j in range(2):
            which = jnp.clip(src_ref[j, g] - blk + 1, 0, 2)
            base, _ = base_of(shift_ref[j, g])
            for i in range(3):
                rows = pl.ds(8 * g + base + i, 8)
                wins.append(
                    jnp.concatenate([ext[which, l, rows, :] for l in range(NLON)], axis=0)
                )
        high, low = halves(jnp.concatenate(wins, axis=1))
        r = dot(jnp.concatenate([high, low], axis=0), toep[g])
        r = r[:, :128] + r[:, 128:]
        r = r[: 8 * NLON] + r[8 * NLON :]
        for l in range(NLON):
            lensed_ref[l, p // 2, pl.ds(16 * g + p % 2, 8, stride=2), :] = r[8 * l : 8 * l + 8]


def kernel(
    spec_ref, src_hbm, shift_hbm, taps_hbm, first_hbm, cos_hbm, sin_hbm, last_hbm,
    plain_ref, lensed_ref,
    ext_0, ext_1, ext_2, ext_3, land, made, toep, src_ref, shift_ref, taps_ref,
    first_ref, cos_ref, sin_ref, last_ref, first_cat, last_cat,
    own_sem, send_a, recv_a, send_b, recv_b, send_c, recv_c,
):
    ext = (ext_0, ext_1, ext_2, ext_3)
    blk = lax.axis_index("blk")
    lon = lax.axis_index("lon")
    odd = lax.rem(blk, 2)
    near = blk + 1 - 2 * odd
    far = blk - 1 + 2 * odd
    has_far = (blk > 0) & (blk < NBLK - 1)

    barrier = pltpu.get_barrier_semaphore()

    def greet(o, carry):
        pl.semaphore_signal(
            barrier, inc=1, device_id=(lax.rem(blk + o, NBLK), lon), device_id_type=MESH
        )
        return carry

    lax.fori_loop(1, NBLK, greet, 0, unroll=9)
    for d in range(1, NLON):
        pl.semaphore_signal(
            barrier, inc=1, device_id=(blk, lax.rem(lon + d, NLON)), device_id_type=MESH
        )

    @pl.when(has_far)
    def _():
        for d in range(1, NLON):
            pl.semaphore_signal(
                barrier, inc=1, device_id=(far, lax.rem(lon + d, NLON)), device_id_type=MESH
            )

    loads = [
        pltpu.make_async_copy(source, target, own_sem.at[j])
        for j, (source, target) in enumerate(
            [(spec_ref.at[blk, p], land.at[p, blk]) for p in range(PARTS)]
            + [
                (src_hbm, src_ref),
                (shift_hbm, shift_ref),
                (taps_hbm, taps_ref.at[pl.ds(0, 16)]),
                (first_hbm, first_ref),
                (cos_hbm, cos_ref),
                (sin_hbm, sin_ref),
                (last_hbm, last_ref),
            ]
        )
    ]
    for load in loads:
        load.start()
    pl.semaphore_wait(
        barrier, NBLK - 1 + (NLON - 1) * (1 + has_far.astype(jnp.int32))
    )

    for p in range(PARTS):

        def send(o, carry, p=p):
            to = 8 * (o // 8) + lax.rem(blk + o, 8)

            @pl.when(to != blk)
            def _():
                pltpu.make_async_remote_copy(
                    src_ref=spec_ref.at[to, p],
                    dst_ref=land.at[p, blk],
                    send_sem=send_a.at[p],
                    recv_sem=recv_a.at[p],
                    device_id=(to, lon),
                    device_id_type=MESH,
                ).start()

            return carry

        lax.fori_loop(0, NBLK, send, 0)

    for load in loads:
        load.wait()
    first_cat[...] = jnp.concatenate(halves(first_ref[...]), axis=0)
    for l in range(NLON):
        last_cat[2 * ROWS * l : 2 * ROWS * (l + 1)] = jnp.concatenate(
            halves(last_ref[ROWS * l : ROWS * (l + 1)]), axis=0
        )
    place_taps(shift_ref, taps_ref, toep)

    others = [land.at[p, pl.ds(0, NBLK - 1)] for p in range(PARTS)]

    def across(p, d):
        to = lax.rem(lon + d, NLON)
        return pltpu.make_async_remote_copy(
            src_ref=made.at[p, to],
            dst_ref=ext[p].at[1, lon],
            send_sem=send_b,
            recv_sem=recv_b.at[p, d],
            device_id=(blk, to),
            device_id_type=MESH,
        )

    def beside(p, source, l, row, to, slot, side):
        pltpu.make_async_remote_copy(
            src_ref=source,
            dst_ref=ext[p].at[slot, l],
            send_sem=send_c.at[side, p],
            recv_sem=recv_c.at[side, p],
            device_id=(row, to),
            device_id_type=MESH,
        ).start()

    def to_near(p, source, l):
        beside(p, source, l, near, lon, 2 * odd, 0)

    def to_far(p, source, l, to):
        @pl.when(has_far)
        def _():
            beside(p, source, l, far, to, 2 - 2 * odd, 1)

    def keep(p):
        return pltpu.make_async_copy(made.at[p, lon], ext[p].at[1, lon], own_sem.at[11 + p])

    def turn(p):
        pltpu.make_async_copy(others[p], others[p], recv_a.at[p]).wait()
        turned = transform(p, land, first_cat, cos_ref, sin_ref)
        for d in (1, 3, 2, 0):
            to = lax.rem(lon + d, NLON)
            made[p, to] = pixels(last_cat, to, turned)
            if d != 0:
                across(p, d).start()
            if d == 0 or p >= DIRECT:
                to_far(p, made.at[p, to], lon, to)
        to_near(p, made.at[p, lon], lon)
        keep(p).start()

    def pass_on(p):
        for d in (1, 3, 2):
            l = lax.rem(lon + NLON - d, NLON)
            across(p, d).wait_recv()
            to_near(p, ext[p].at[1, l], l)
            if p < DIRECT:
                to_far(p, ext[p].at[1, l], l, lon)

    def finish_part(p):
        keep(p).wait()
        for l in range(NLON):
            plain_ref[l, p // 2, pl.ds(p % 2, 64, stride=2), :] = ext[p][1, l, 4:68, :]
        rows = ext[p].at[0]
        pltpu.make_async_copy(rows, rows, recv_c.at[0, p]).wait()

        @pl.when(has_far)
        def _():
            pltpu.make_async_copy(rows, rows, recv_c.at[1, p]).wait()

        lens(p, blk, src_ref, shift_ref, ext[p], toep, lensed_ref)

    def sent(p):
        rows = ext[p].at[0]
        pltpu.make_async_copy(rows, rows, send_c.at[0, p]).wait()

        @pl.when(has_far)
        def _():
            pltpu.make_async_copy(rows, rows, send_c.at[1, p]).wait()

        pltpu.make_async_copy(others[p], others[p], send_a.at[p]).wait()

    turn(0)
    turn(1)
    pass_on(0)
    turn(2)
    pass_on(1)
    turn(3)
    finish_part(0)
    pass_on(2)
    finish_part(1)
    pass_on(3)
    finish_part(2)
    for p in range(3):
        sent(p)
    every = made.at[:, pl.ds(0, NLON - 1)]
    pltpu.make_async_copy(every, every, send_b).wait()
    finish_part(3)
    sent(3)


def finish(plain_vmem, lensed_vmem, plain_ref, lensed_ref, sems):
    copies = [
        pltpu.make_async_copy(source.at[l], target.at[l], sems.at[j, l])
        for j, (source, target) in enumerate(((plain_vmem, plain_ref), (lensed_vmem, lensed_ref)))
        for l in range(NLON)
    ]
    for copy in copies:
        copy.start()
    for copy in copies:
        copy.wait()


def shards(spectra, source_tiles, tap_shift, kernels):
    spec = spectra.reshape(NBLK, 2, 2, 2, 2, 128).transpose(0, 1, 2, 4, 3, 5)
    operands = (
        spec.reshape(NBLK, PARTS, 4, 128),
        source_tiles.transpose(0, 2, 1).reshape(2, 8),
        tap_shift.transpose(0, 2, 1).reshape(2, 8),
        kernels.reshape(16, 128),
        *map(jnp.asarray, tables()),
    )
    vmem = pl.BlockSpec(memory_space=pltpu.VMEM)
    hbm = pl.BlockSpec(memory_space=pltpu.HBM)
    dma = pltpu.SemaphoreType.DMA
    shape = jax.ShapeDtypeStruct((NLON, 2, 128, 128), F32)
    maps_in_vmem = pl.pallas_call(
        kernel,
        out_shape=(shape, shape),
        in_specs=[hbm] * 8,
        out_specs=(vmem, vmem),
        scratch_shapes=[pltpu.VMEM((3, NLON, ROWS, 128), F32)] * PARTS
        + [
            pltpu.VMEM((PARTS, NBLK, 4, 128), F32),
            pltpu.VMEM((PARTS, NLON, ROWS, 128), F32),
            pltpu.VMEM((8, 768, 256), BF16),
            pltpu.SMEM((2, 8), jnp.int32),
            pltpu.SMEM((2, 8), jnp.int32),
            pltpu.VMEM((32, 128), F32),
            pltpu.VMEM((512, 256), F32),
            pltpu.VMEM((128, 256), F32),
            pltpu.VMEM((128, 256), F32),
            pltpu.VMEM((NLON * ROWS, 512), F32),
            pltpu.VMEM((1024, 256), BF16),
            pltpu.VMEM((2 * NLON * ROWS, 512), BF16),
            dma((11 + PARTS,)),
            dma((PARTS,)),
            dma((PARTS,)),
            dma,
            dma((PARTS, NLON)),
            dma((2, PARTS)),
            dma((2, PARTS)),
        ],
        compiler_params=pltpu.CompilerParams(
            collective_id=0, has_side_effects=True, vmem_limit_bytes=32 * 1024 * 1024
        ),
    )(*(pltpu.with_memory_space_constraint(x, pltpu.HBM) for x in operands))
    plain, lensed = pl.pallas_call(
        finish,
        out_shape=(shape, shape),
        in_specs=[vmem, vmem],
        out_specs=(hbm, hbm),
        scratch_shapes=[dma((2, NLON))],
        compiler_params=pltpu.CompilerParams(vmem_limit_bytes=16 * 1024 * 1024),
    )(*maps_in_vmem)

    def maps(x):
        return x.reshape(8, 64, 2, 128).transpose(0, 2, 1, 3).reshape(8, 2, 8192)

    return maps(plain), maps(lensed)


def solution(mesh):
    placed = (
        P(None, "lon", None, None, None, "blk"),
        P("blk", "lon", None),
        P("blk", "lon", None),
        P("blk", "lon", None, None),
    )
    return jax.shard_map(
        shards,
        mesh=mesh,
        in_specs=placed,
        out_specs=(P("blk", None, "lon"), P("blk", None, "lon")),
        check_vma=False,
    )
```

```python
import math

import jax
import jax.numpy as jnp
import numpy as np
from jax import lax
from jax.experimental import pallas as pl
from jax.experimental.pallas import tpu as pltpu
from jax.sharding import PartitionSpec as P

NBLK = 64
NLON = 4
PARTS = 4
DIRECT = 2
MESH = pl.DeviceIdType.MESH
F32 = jnp.float32
BF16 = jnp.bfloat16

ROWS = 72


def tables():
    def angle(rows, cols, period):
        return 2.0 * math.pi * ((rows[:, None] * cols[None, :]) % period) / period

    i = np.arange(128)
    b = np.arange(NBLK)
    n = np.arange(256)
    turn = angle(i, b, 128)
    first = np.zeros((2, 2, 128, NBLK, 2, 2))
    for h in range(2):
        first[h, 0, :, :, h, 0] = np.cos(turn)
        first[h, 0, :, :, h, 1] = -np.sin(turn)
        first[h, 1, :, :, h, 0] = np.sin(turn)
        first[h, 1, :, :, h, 1] = np.cos(turn)
    first = first.reshape(512, 256)
    turn = angle(i, n, 32768)
    pixel_rows = np.concatenate([(64 * l + np.arange(ROWS) - 4) % 256 for l in range(NLON)])
    last = angle(pixel_rows, n, 256)
    last = np.concatenate([np.cos(last), -np.sin(last)], axis=1)
    return tuple(t.astype(np.float32) for t in (first, np.cos(turn), np.sin(turn), last))


def halves(x):
    high = x.astype(BF16)
    return high, (x - high.astype(F32)).astype(BF16)


def dot(a, b):
    return jnp.dot(a, b, preferred_element_type=F32)


def nt(a, b):
    return lax.dot_general(a, b, (((1,), (1,)), ((), ())), preferred_element_type=F32)


def transform(p, land, first_ref, cos_ref, sin_ref):
    x = jnp.concatenate(halves(land[p].reshape(4 * NBLK, 128)), axis=1)
    r = dot(first_ref[...], x)
    g = r[:512, :128] + (r[:512, 128:] + r[512:, :128])
    real, imag = [], []
    for h in range(2):
        gre, gim = g[256 * h : 256 * h + 128], g[256 * h + 128 : 256 * h + 256]
        cos, sin = cos_ref[:, 128 * h : 128 * h + 128], sin_ref[:, 128 * h : 128 * h + 128]
        real.append(gre * cos - gim * sin)
        imag.append(gre * sin + gim * cos)
    return jnp.concatenate(halves(jnp.concatenate(real + imag, axis=1)), axis=0)


def pixels(last_ref, l, turned):
    r = nt(last_ref[pl.ds(pl.multiple_of(2 * ROWS * l, 16), 2 * ROWS), :], turned)
    return r[:ROWS, :128] + (r[:ROWS, 128:] + r[ROWS:, :128])


def base_of(shift):
    start = shift + 448
    base = jnp.clip(lax.shift_right_arithmetic(start, 7), 0, 6)
    return base, start - 128 * base


def place_taps(shift_ref, taps_ref, toep):
    lane = lax.broadcasted_iota(jnp.int32, (128, 128), 1)
    row = lax.broadcasted_iota(jnp.int32, (128, 128), 0)
    lead = row - lane
    flip = jnp.where(row + lane == 127, 1.0, 0.0).astype(BF16)
    high, low = halves(taps_ref[:16])
    taps_ref[...] = jnp.concatenate([dot(high, flip), dot(low, flip)], axis=0)

    def one(g, carry):
        for j in range(2):
            _, off = base_of(shift_ref[j, g])
            for half in range(2):
                taps = taps_ref[pl.ds(16 * half + 2 * g + j, 1), :]
                taps = pltpu.roll(jnp.broadcast_to(taps, (8, 128)), (129 - off) & 127, 1)
                ring = pltpu.roll(
                    jnp.broadcast_to(taps[:1], (128, 128)), 0, 1, stride=1, stride_axis=0
                )
                for i in range(3):
                    at = lead + (128 * i - off)
                    rows = slice(384 * j + 128 * i, 384 * j + 128 * i + 128)
                    toep[g, rows, 128 * half : 128 * half + 128] = jnp.where(
                        (at >= 0) & (at < 128), ring, 0.0
                    ).astype(BF16)
        return carry

    lax.fori_loop(0, 8, one, 0)


def lens(p, blk, src_ref, shift_ref, ext, toep, lensed_ref):
    for g in range(8):
        wins = []
        for j in range(2):
            which = jnp.clip(src_ref[j, g] - blk + 1, 0, 2)
            base, _ = base_of(shift_ref[j, g])
            for i in range(3):
                rows = pl.ds(8 * g + base + i, 8)
                wins.append(
                    jnp.concatenate([ext[which, l, rows, :] for l in range(NLON)], axis=0)
                )
        high, low = halves(jnp.concatenate(wins, axis=1))
        r = dot(jnp.concatenate([high, low], axis=0), toep[g])
        r = r[:, :128] + r[:, 128:]
        r = r[: 8 * NLON] + r[8 * NLON :]
        for l in range(NLON):
            lensed_ref[l, p // 2, pl.ds(16 * g + p % 2, 8, stride=2), :] = r[8 * l : 8 * l + 8]


def kernel(
    spec_ref, src_hbm, shift_hbm, taps_hbm, first_hbm, cos_hbm, sin_hbm, last_hbm,
    plain_ref, lensed_ref,
    ext_0, ext_1, ext_2, ext_3, land, made, toep, src_ref, shift_ref, taps_ref,
    first_ref, cos_ref, sin_ref, last_ref, first_cat, last_cat,
    own_sem, send_a, recv_a, send_b, recv_b, send_c, recv_c,
):
    ext = (ext_0, ext_1, ext_2, ext_3)
    blk = lax.axis_index("blk")
    lon = lax.axis_index("lon")
    odd = lax.rem(blk, 2)
    near = blk + 1 - 2 * odd
    far = blk - 1 + 2 * odd
    has_far = (blk > 0) & (blk < NBLK - 1)

    barrier = pltpu.get_barrier_semaphore()

    def greet(o, carry):
        pl.semaphore_signal(
            barrier, inc=1, device_id=(lax.rem(blk + o, NBLK), lon), device_id_type=MESH
        )
        return carry

    lax.fori_loop(1, NBLK, greet, 0, unroll=9)
    for d in range(1, NLON):
        pl.semaphore_signal(
            barrier, inc=1, device_id=(blk, lax.rem(lon + d, NLON)), device_id_type=MESH
        )

    @pl.when(has_far)
    def _():
        for d in range(1, NLON):
            pl.semaphore_signal(
                barrier, inc=1, device_id=(far, lax.rem(lon + d, NLON)), device_id_type=MESH
            )

    loads = [
        pltpu.make_async_copy(source, target, own_sem.at[j])
        for j, (source, target) in enumerate(
            [(spec_ref.at[blk, p], land.at[p, blk]) for p in range(PARTS)]
            + [
                (src_hbm, src_ref),
                (shift_hbm, shift_ref),
                (taps_hbm, taps_ref.at[pl.ds(0, 16)]),
                (first_hbm, first_ref),
                (cos_hbm, cos_ref),
                (sin_hbm, sin_ref),
                (last_hbm, last_ref),
            ]
        )
    ]
    for load in loads:
        load.start()
    pl.semaphore_wait(
        barrier, NBLK - 1 + (NLON - 1) * (1 + has_far.astype(jnp.int32))
    )

    def send_spectra(p):
        def one(to):
            pltpu.make_async_remote_copy(
                src_ref=spec_ref.at[to, p],
                dst_ref=land.at[p, blk],
                send_sem=send_a.at[p],
                recv_sem=recv_a.at[p],
                device_id=(to, lon),
                device_id_type=MESH,
            ).start()

        def send(plane, carry):
            @pl.when(plane != blk // 8)
            def _():
                one(8 * plane + lax.rem(blk, 8))

            for step in range(1, 8):
                one(8 * plane + lax.rem(blk + step, 8))
            return carry

        lax.fori_loop(0, NBLK // 8, send, 0)

    def prepare():
        for load in loads:
            load.wait()
        first_cat[...] = jnp.concatenate(halves(first_ref[...]), axis=0)
        for l in range(NLON):
            last_cat[2 * ROWS * l : 2 * ROWS * (l + 1)] = jnp.concatenate(
                halves(last_ref[ROWS * l : ROWS * (l + 1)]), axis=0
            )

    others = [land.at[p, pl.ds(0, NBLK - 1)] for p in range(PARTS)]

    def across(p, d):
        to = lax.rem(lon + d, NLON)
        return pltpu.make_async_remote_copy(
            src_ref=made.at[p, to],
            dst_ref=ext[p].at[1, lon],
            send_sem=send_b,
            recv_sem=recv_b.at[p, d],
            device_id=(blk, to),
            device_id_type=MESH,
        )

    def beside(p, source, l, row, to, slot, side):
        pltpu.make_async_remote_copy(
            src_ref=source,
            dst_ref=ext[p].at[slot, l],
            send_sem=send_c.at[side, p],
            recv_sem=recv_c.at[side, p],
            device_id=(row, to),
            device_id_type=MESH,
        ).start()

    def to_near(p, source, l):
        beside(p, source, l, near, lon, 2 * odd, 0)

    def to_far(p, source, l, to):
        @pl.when(has_far)
        def _():
            beside(p, source, l, far, to, 2 - 2 * odd, 1)

    def keep(p):
        return pltpu.make_async_copy(made.at[p, lon], ext[p].at[1, lon], own_sem.at[11 + p])

    def turn(p):
        pltpu.make_async_copy(others[p], others[p], recv_a.at[p]).wait()
        turned = transform(p, land, first_cat, cos_ref, sin_ref)
        for d in (1, 3, 2, 0):
            to = lax.rem(lon + d, NLON)
            made[p, to] = pixels(last_cat, to, turned)
            if d != 0:
                across(p, d).start()
            if d == 0 or p >= DIRECT:
                to_far(p, made.at[p, to], lon, to)
        to_near(p, made.at[p, lon], lon)
        keep(p).start()

    def pass_on(p):
        for d in (1, 3, 2):
            l = lax.rem(lon + NLON - d, NLON)
            across(p, d).wait_recv()
            to_near(p, ext[p].at[1, l], l)
            if p < DIRECT:
                to_far(p, ext[p].at[1, l], l, lon)

    def finish_part(p):
        keep(p).wait()
        for l in range(NLON):
            plain_ref[l, p // 2, pl.ds(p % 2, 64, stride=2), :] = ext[p][1, l, 4:68, :]
        rows = ext[p].at[0]
        pltpu.make_async_copy(rows, rows, recv_c.at[0, p]).wait()

        @pl.when(has_far)
        def _():
            pltpu.make_async_copy(rows, rows, recv_c.at[1, p]).wait()

        lens(p, blk, src_ref, shift_ref, ext[p], toep, lensed_ref)

    def sent(p):
        rows = ext[p].at[0]
        pltpu.make_async_copy(rows, rows, send_c.at[0, p]).wait()

        @pl.when(has_far)
        def _():
            pltpu.make_async_copy(rows, rows, send_c.at[1, p]).wait()

        pltpu.make_async_copy(others[p], others[p], send_a.at[p]).wait()

    for p in range(PARTS):
        send_spectra(p)
    prepare()
    place_taps(shift_ref, taps_ref, toep)
    turn(0)
    turn(1)
    pass_on(0)
    turn(2)
    pass_on(1)
    turn(3)
    finish_part(0)
    pass_on(2)
    finish_part(1)
    pass_on(3)
    finish_part(2)
    for p in range(3):
        sent(p)
    every = made.at[:, pl.ds(0, NLON - 1)]
    pltpu.make_async_copy(every, every, send_b).wait()
    finish_part(3)
    sent(3)


def finish(plain_vmem, lensed_vmem, plain_ref, lensed_ref, sems):
    copies = [
        pltpu.make_async_copy(source.at[l], target.at[l], sems.at[j, l])
        for j, (source, target) in enumerate(((plain_vmem, plain_ref), (lensed_vmem, lensed_ref)))
        for l in range(NLON)
    ]
    for copy in copies:
        copy.start()
    for copy in copies:
        copy.wait()


def shards(spectra, source_tiles, tap_shift, kernels):
    spec = spectra.reshape(NBLK, 2, 2, 2, 2, 128).transpose(0, 1, 2, 4, 3, 5)
    operands = (
        spec.reshape(NBLK, PARTS, 4, 128),
        source_tiles.transpose(0, 2, 1).reshape(2, 8),
        tap_shift.transpose(0, 2, 1).reshape(2, 8),
        kernels.reshape(16, 128),
        *map(jnp.asarray, tables()),
    )
    vmem = pl.BlockSpec(memory_space=pltpu.VMEM)
    hbm = pl.BlockSpec(memory_space=pltpu.HBM)
    dma = pltpu.SemaphoreType.DMA
    shape = jax.ShapeDtypeStruct((NLON, 2, 128, 128), F32)
    maps_in_vmem = pl.pallas_call(
        kernel,
        out_shape=(shape, shape),
        in_specs=[hbm] * 8,
        out_specs=(vmem, vmem),
        scratch_shapes=[pltpu.VMEM((3, NLON, ROWS, 128), F32)] * PARTS
        + [
            pltpu.VMEM((PARTS, NBLK, 4, 128), F32),
            pltpu.VMEM((PARTS, NLON, ROWS, 128), F32),
            pltpu.VMEM((8, 768, 256), BF16),
            pltpu.SMEM((2, 8), jnp.int32),
            pltpu.SMEM((2, 8), jnp.int32),
            pltpu.VMEM((32, 128), F32),
            pltpu.VMEM((512, 256), F32),
            pltpu.VMEM((128, 256), F32),
            pltpu.VMEM((128, 256), F32),
            pltpu.VMEM((NLON * ROWS, 512), F32),
            pltpu.VMEM((1024, 256), BF16),
            pltpu.VMEM((2 * NLON * ROWS, 512), BF16),
            dma((11 + PARTS,)),
            dma((PARTS,)),
            dma((PARTS,)),
            dma,
            dma((PARTS, NLON)),
            dma((2, PARTS)),
            dma((2, PARTS)),
        ],
        compiler_params=pltpu.CompilerParams(
            collective_id=0, has_side_effects=True, vmem_limit_bytes=32 * 1024 * 1024
        ),
    )(*(pltpu.with_memory_space_constraint(x, pltpu.HBM) for x in operands))
    plain, lensed = pl.pallas_call(
        finish,
        out_shape=(shape, shape),
        in_specs=[vmem, vmem],
        out_specs=(hbm, hbm),
        scratch_shapes=[dma((2, NLON))],
        compiler_params=pltpu.CompilerParams(vmem_limit_bytes=16 * 1024 * 1024),
    )(*maps_in_vmem)

    def maps(x):
        return x.reshape(8, 64, 2, 128).transpose(0, 2, 1, 3).reshape(8, 2, 8192)

    return maps(plain), maps(lensed)


def solution(mesh):
    placed = (
        P(None, "lon", None, None, None, "blk"),
        P("blk", "lon", None),
        P("blk", "lon", None),
        P("blk", "lon", None, None),
    )
    return jax.shard_map(
        shards,
        mesh=mesh,
        in_specs=placed,
        out_specs=(P("blk", None, "lon"), P("blk", None, "lon")),
        check_vma=False,
    )
```

```python
import math

import jax
import jax.numpy as jnp
import numpy as np
from jax import lax
from jax.experimental import pallas as pl
from jax.experimental.pallas import tpu as pltpu
from jax.sharding import PartitionSpec as P

NBLK = 64
NLON = 4
PARTS = 4
DIRECT = 2
MESH = pl.DeviceIdType.MESH
F32 = jnp.float32
BF16 = jnp.bfloat16

ROWS = 72


def tables():
    def angle(rows, cols, period):
        return 2.0 * math.pi * ((rows[:, None] * cols[None, :]) % period) / period

    i = np.arange(128)
    b = np.arange(NBLK)
    n = np.arange(256)
    turn = angle(i, b, 128)
    first = np.zeros((2, 2, 128, NBLK, 2, 2))
    for h in range(2):
        first[h, 0, :, :, h, 0] = np.cos(turn)
        first[h, 0, :, :, h, 1] = -np.sin(turn)
        first[h, 1, :, :, h, 0] = np.sin(turn)
        first[h, 1, :, :, h, 1] = np.cos(turn)
    first = first.reshape(512, 256)
    turn = angle(i, n, 32768)
    pixel_rows = np.concatenate([(64 * l + np.arange(ROWS) - 4) % 256 for l in range(NLON)])
    last = angle(pixel_rows, n, 256)
    last = np.concatenate([np.cos(last), -np.sin(last)], axis=1)
    return tuple(t.astype(np.float32) for t in (first, np.cos(turn), np.sin(turn), last))


def halves(x):
    high = x.astype(BF16)
    return high, (x - high.astype(F32)).astype(BF16)


def dot(a, b):
    return jnp.dot(a, b, preferred_element_type=F32)


def nt(a, b):
    return lax.dot_general(a, b, (((1,), (1,)), ((), ())), preferred_element_type=F32)


def transform(p, land, first_ref, cos_ref, sin_ref):
    x = jnp.concatenate(halves(land[p].reshape(4 * NBLK, 128)), axis=1)
    r = dot(first_ref[...], x)
    g = r[:512, :128] + (r[:512, 128:] + r[512:, :128])
    real, imag = [], []
    for h in range(2):
        gre, gim = g[256 * h : 256 * h + 128], g[256 * h + 128 : 256 * h + 256]
        cos, sin = cos_ref[:, 128 * h : 128 * h + 128], sin_ref[:, 128 * h : 128 * h + 128]
        real.append(gre * cos - gim * sin)
        imag.append(gre * sin + gim * cos)
    return jnp.concatenate(halves(jnp.concatenate(real + imag, axis=1)), axis=0)


def pixels(last_ref, l, turned):
    r = nt(last_ref[pl.ds(pl.multiple_of(2 * ROWS * l, 16), 2 * ROWS), :], turned)
    return r[:ROWS, :128] + (r[:ROWS, 128:] + r[ROWS:, :128])


def base_of(shift):
    start = shift + 448
    base = jnp.clip(lax.shift_right_arithmetic(start, 7), 0, 6)
    return base, start - 128 * base


def place_taps(shift_ref, taps_ref, toep):
    lane = lax.broadcasted_iota(jnp.int32, (128, 128), 1)
    row = lax.broadcasted_iota(jnp.int32, (128, 128), 0)
    lead = row - lane
    flip = jnp.where(row + lane == 127, 1.0, 0.0).astype(BF16)
    high, low = halves(taps_ref[:16])
    taps_ref[...] = jnp.concatenate([dot(high, flip), dot(low, flip)], axis=0)

    def one(g, carry):
        for j in range(2):
            _, off = base_of(shift_ref[j, g])
            for half in range(2):
                taps = taps_ref[pl.ds(16 * half + 2 * g + j, 1), :]
                taps = pltpu.roll(jnp.broadcast_to(taps, (8, 128)), (129 - off) & 127, 1)
                ring = pltpu.roll(
                    jnp.broadcast_to(taps[:1], (128, 128)), 0, 1, stride=1, stride_axis=0
                )
                for i in range(3):
                    at = lead + (128 * i - off)
                    rows = slice(384 * j + 128 * i, 384 * j + 128 * i + 128)
                    toep[g, rows, 128 * half : 128 * half + 128] = jnp.where(
                        (at >= 0) & (at < 128), ring, 0.0
                    ).astype(BF16)
        return carry

    lax.fori_loop(0, 8, one, 0)


def lens(p, blk, src_ref, shift_ref, ext, toep, lensed_ref):
    for g in range(8):
        wins = []
        for j in range(2):
            which = jnp.clip(src_ref[j, g] - blk + 1, 0, 2)
            base, _ = base_of(shift_ref[j, g])
            for i in range(3):
                rows = pl.ds(8 * g + base + i, 8)
                wins.append(
                    jnp.concatenate([ext[which, l, rows, :] for l in range(NLON)], axis=0)
                )
        high, low = halves(jnp.concatenate(wins, axis=1))
        r = dot(jnp.concatenate([high, low], axis=0), toep[g])
        r = r[:, :128] + r[:, 128:]
        r = r[: 8 * NLON] + r[8 * NLON :]
        for l in range(NLON):
            lensed_ref[l, p // 2, pl.ds(16 * g + p % 2, 8, stride=2), :] = r[8 * l : 8 * l + 8]


def kernel(
    spec_ref, src_hbm, shift_hbm, taps_hbm, first_hbm, cos_hbm, sin_hbm, last_hbm,
    plain_ref, lensed_ref,
    ext_0, ext_1, ext_2, ext_3, land, made, toep, src_ref, shift_ref, taps_ref,
    first_ref, cos_ref, sin_ref, last_ref, first_cat, last_cat,
    own_sem, send_a, recv_a, send_b, recv_b, send_c, recv_c,
):
    ext = (ext_0, ext_1, ext_2, ext_3)
    blk = lax.axis_index("blk")
    lon = lax.axis_index("lon")
    odd = lax.rem(blk, 2)
    near = blk + 1 - 2 * odd
    far = blk - 1 + 2 * odd
    has_far = (blk > 0) & (blk < NBLK - 1)

    barrier = pltpu.get_barrier_semaphore()

    def greet(o, carry):
        pl.semaphore_signal(
            barrier, inc=1, device_id=(lax.rem(blk + o, NBLK), lon), device_id_type=MESH
        )
        return carry

    lax.fori_loop(1, NBLK, greet, 0, unroll=9)
    for d in range(1, NLON):
        pl.semaphore_signal(
            barrier, inc=1, device_id=(blk, lax.rem(lon + d, NLON)), device_id_type=MESH
        )

    @pl.when(has_far)
    def _():
        for d in range(1, NLON):
            pl.semaphore_signal(
                barrier, inc=1, device_id=(far, lax.rem(lon + d, NLON)), device_id_type=MESH
            )

    loads = [
        pltpu.make_async_copy(source, target, own_sem.at[j])
        for j, (source, target) in enumerate(
            [(spec_ref.at[blk, p], land.at[p, blk]) for p in range(PARTS)]
            + [
                (src_hbm, src_ref),
                (shift_hbm, shift_ref),
                (taps_hbm, taps_ref.at[pl.ds(0, 16)]),
                (first_hbm, first_ref),
                (cos_hbm, cos_ref),
                (sin_hbm, sin_ref),
                (last_hbm, last_ref),
            ]
        )
    ]
    for load in loads:
        load.start()
    def prepare():
        for load in loads:
            load.wait()
        first_cat[...] = jnp.concatenate(halves(first_ref[...]), axis=0)
        for l in range(NLON):
            last_cat[2 * ROWS * l : 2 * ROWS * (l + 1)] = jnp.concatenate(
                halves(last_ref[ROWS * l : ROWS * (l + 1)]), axis=0
            )
        place_taps(shift_ref, taps_ref, toep)

    pl.when(blk < NBLK // 2)(prepare)
    pl.semaphore_wait(
        barrier, NBLK - 1 + (NLON - 1) * (1 + has_far.astype(jnp.int32))
    )

    for p in range(PARTS):

        def send(o, carry, p=p):
            to = 8 * (o // 8) + lax.rem(blk + o, 8)

            @pl.when(to != blk)
            def _():
                pltpu.make_async_remote_copy(
                    src_ref=spec_ref.at[to, p],
                    dst_ref=land.at[p, blk],
                    send_sem=send_a.at[p],
                    recv_sem=recv_a.at[p],
                    device_id=(to, lon),
                    device_id_type=MESH,
                ).start()

            return carry

        lax.fori_loop(0, NBLK, send, 0)

    pl.when(blk >= NBLK // 2)(prepare)

    others = [land.at[p, pl.ds(0, NBLK - 1)] for p in range(PARTS)]

    def across(p, d):
        to = lax.rem(lon + d, NLON)
        return pltpu.make_async_remote_copy(
            src_ref=made.at[p, to],
            dst_ref=ext[p].at[1, lon],
            send_sem=send_b,
            recv_sem=recv_b.at[p, d],
            device_id=(blk, to),
            device_id_type=MESH,
        )

    def beside(p, source, l, row, to, slot, side):
        pltpu.make_async_remote_copy(
            src_ref=source,
            dst_ref=ext[p].at[slot, l],
            send_sem=send_c.at[side, p],
            recv_sem=recv_c.at[side, p],
            device_id=(row, to),
            device_id_type=MESH,
        ).start()

    def to_near(p, source, l):
        beside(p, source, l, near, lon, 2 * odd, 0)

    def to_far(p, source, l, to):
        @pl.when(has_far)
        def _():
            beside(p, source, l, far, to, 2 - 2 * odd, 1)

    def keep(p):
        return pltpu.make_async_copy(made.at[p, lon], ext[p].at[1, lon], own_sem.at[11 + p])

    def turn(p):
        pltpu.make_async_copy(others[p], others[p], recv_a.at[p]).wait()
        turned = transform(p, land, first_cat, cos_ref, sin_ref)
        for d in (1, 3, 2, 0):
            to = lax.rem(lon + d, NLON)
            made[p, to] = pixels(last_cat, to, turned)
            if d != 0:
                across(p, d).start()
            if d == 0 or p >= DIRECT:
                to_far(p, made.at[p, to], lon, to)
        to_near(p, made.at[p, lon], lon)
        keep(p).start()

    def pass_on(p):
        for d in (1, 3, 2):
            l = lax.rem(lon + NLON - d, NLON)
            across(p, d).wait_recv()
            to_near(p, ext[p].at[1, l], l)
            if p < DIRECT:
                to_far(p, ext[p].at[1, l], l, lon)

    def finish_part(p):
        keep(p).wait()
        for l in range(NLON):
            plain_ref[l, p // 2, pl.ds(p % 2, 64, stride=2), :] = ext[p][1, l, 4:68, :]
        rows = ext[p].at[0]
        pltpu.make_async_copy(rows, rows, recv_c.at[0, p]).wait()

        @pl.when(has_far)
        def _():
            pltpu.make_async_copy(rows, rows, recv_c.at[1, p]).wait()

        lens(p, blk, src_ref, shift_ref, ext[p], toep, lensed_ref)

    def sent(p):
        rows = ext[p].at[0]
        pltpu.make_async_copy(rows, rows, send_c.at[0, p]).wait()

        @pl.when(has_far)
        def _():
            pltpu.make_async_copy(rows, rows, send_c.at[1, p]).wait()

        pltpu.make_async_copy(others[p], others[p], send_a.at[p]).wait()

    turn(0)
    turn(1)
    pass_on(0)
    turn(2)
    pass_on(1)
    turn(3)
    finish_part(0)
    pass_on(2)
    finish_part(1)
    pass_on(3)
    finish_part(2)
    for p in range(3):
        sent(p)
    every = made.at[:, pl.ds(0, NLON - 1)]
    pltpu.make_async_copy(every, every, send_b).wait()
    finish_part(3)
    sent(3)


def finish(plain_vmem, lensed_vmem, plain_ref, lensed_ref, sems):
    copies = [
        pltpu.make_async_copy(source.at[l], target.at[l], sems.at[j, l])
        for j, (source, target) in enumerate(((plain_vmem, plain_ref), (lensed_vmem, lensed_ref)))
        for l in range(NLON)
    ]
    for copy in copies:
        copy.start()
    for copy in copies:
        copy.wait()


def shards(spectra, source_tiles, tap_shift, kernels):
    spec = spectra.reshape(NBLK, 2, 2, 2, 2, 128).transpose(0, 1, 2, 4, 3, 5)
    operands = (
        spec.reshape(NBLK, PARTS, 4, 128),
        source_tiles.transpose(0, 2, 1).reshape(2, 8),
        tap_shift.transpose(0, 2, 1).reshape(2, 8),
        kernels.reshape(16, 128),
        *map(jnp.asarray, tables()),
    )
    vmem = pl.BlockSpec(memory_space=pltpu.VMEM)
    hbm = pl.BlockSpec(memory_space=pltpu.HBM)
    dma = pltpu.SemaphoreType.DMA
    shape = jax.ShapeDtypeStruct((NLON, 2, 128, 128), F32)
    maps_in_vmem = pl.pallas_call(
        kernel,
        out_shape=(shape, shape),
        in_specs=[hbm] * 8,
        out_specs=(vmem, vmem),
        scratch_shapes=[pltpu.VMEM((3, NLON, ROWS, 128), F32)] * PARTS
        + [
            pltpu.VMEM((PARTS, NBLK, 4, 128), F32),
            pltpu.VMEM((PARTS, NLON, ROWS, 128), F32),
            pltpu.VMEM((8, 768, 256), BF16),
            pltpu.SMEM((2, 8), jnp.int32),
            pltpu.SMEM((2, 8), jnp.int32),
            pltpu.VMEM((32, 128), F32),
            pltpu.VMEM((512, 256), F32),
            pltpu.VMEM((128, 256), F32),
            pltpu.VMEM((128, 256), F32),
            pltpu.VMEM((NLON * ROWS, 512), F32),
            pltpu.VMEM((1024, 256), BF16),
            pltpu.VMEM((2 * NLON * ROWS, 512), BF16),
            dma((11 + PARTS,)),
            dma((PARTS,)),
            dma((PARTS,)),
            dma,
            dma((PARTS, NLON)),
            dma((2, PARTS)),
            dma((2, PARTS)),
        ],
        compiler_params=pltpu.CompilerParams(
            collective_id=0, has_side_effects=True, vmem_limit_bytes=32 * 1024 * 1024
        ),
    )(*(pltpu.with_memory_space_constraint(x, pltpu.HBM) for x in operands))
    plain, lensed = pl.pallas_call(
        finish,
        out_shape=(shape, shape),
        in_specs=[vmem, vmem],
        out_specs=(hbm, hbm),
        scratch_shapes=[dma((2, NLON))],
        compiler_params=pltpu.CompilerParams(vmem_limit_bytes=16 * 1024 * 1024),
    )(*maps_in_vmem)

    def maps(x):
        return x.reshape(8, 64, 2, 128).transpose(0, 2, 1, 3).reshape(8, 2, 8192)

    return maps(plain), maps(lensed)


def solution(mesh):
    placed = (
        P(None, "lon", None, None, None, "blk"),
        P("blk", "lon", None),
        P("blk", "lon", None),
        P("blk", "lon", None, None),
    )
    return jax.shard_map(
        shards,
        mesh=mesh,
        in_specs=placed,
        out_specs=(P("blk", None, "lon"), P("blk", None, "lon")),
        check_vma=False,
    )
```

```python
import math

import jax
import jax.numpy as jnp
import numpy as np
from jax import lax
from jax.experimental import pallas as pl
from jax.experimental.pallas import tpu as pltpu
from jax.sharding import PartitionSpec as P

NBLK = 64
NLON = 4
PARTS = 4
DIRECT = 2
MESH = pl.DeviceIdType.MESH
F32 = jnp.float32
BF16 = jnp.bfloat16

ROWS = 72


def tables():
    def angle(rows, cols, period):
        return 2.0 * math.pi * ((rows[:, None] * cols[None, :]) % period) / period

    i = np.arange(128)
    b = np.arange(NBLK)
    n = np.arange(256)
    turn = angle(i, b, 128)
    first = np.zeros((2, 2, 128, NBLK, 2, 2))
    for h in range(2):
        first[h, 0, :, :, h, 0] = np.cos(turn)
        first[h, 0, :, :, h, 1] = -np.sin(turn)
        first[h, 1, :, :, h, 0] = np.sin(turn)
        first[h, 1, :, :, h, 1] = np.cos(turn)
    first = first.reshape(512, 256)
    turn = angle(i, n, 32768)
    pixel_rows = np.concatenate([(64 * l + np.arange(ROWS) - 4) % 256 for l in range(NLON)])
    last = angle(pixel_rows, n, 256)
    last = np.concatenate([np.cos(last), -np.sin(last)], axis=1)
    return tuple(t.astype(np.float32) for t in (first, np.cos(turn), np.sin(turn), last))


def halves(x):
    high = x.astype(BF16)
    return high, (x - high.astype(F32)).astype(BF16)


def dot(a, b):
    return jnp.dot(a, b, preferred_element_type=F32)


def nt(a, b):
    return lax.dot_general(a, b, (((1,), (1,)), ((), ())), preferred_element_type=F32)


def transform(p, land, first_ref, cos_ref, sin_ref):
    x = jnp.concatenate(halves(land[p].reshape(4 * NBLK, 128)), axis=1)
    r = dot(first_ref[...], x)
    g = r[:512, :128] + (r[:512, 128:] + r[512:, :128])
    real, imag = [], []
    for h in range(2):
        gre, gim = g[256 * h : 256 * h + 128], g[256 * h + 128 : 256 * h + 256]
        cos, sin = cos_ref[:, 128 * h : 128 * h + 128], sin_ref[:, 128 * h : 128 * h + 128]
        real.append(gre * cos - gim * sin)
        imag.append(gre * sin + gim * cos)
    return jnp.concatenate(halves(jnp.concatenate(real + imag, axis=1)), axis=0)


def pixels(last_ref, l, turned):
    r = nt(last_ref[pl.ds(pl.multiple_of(2 * ROWS * l, 16), 2 * ROWS), :], turned)
    return r[:ROWS, :128] + (r[:ROWS, 128:] + r[ROWS:, :128])


def base_of(shift):
    start = shift + 448
    base = jnp.clip(lax.shift_right_arithmetic(start, 7), 0, 6)
    return base, start - 128 * base


def place_taps(shift_ref, taps_ref, toep):
    lane = lax.broadcasted_iota(jnp.int32, (128, 128), 1)
    row = lax.broadcasted_iota(jnp.int32, (128, 128), 0)
    lead = row - lane
    flip = jnp.where(row + lane == 127, 1.0, 0.0).astype(BF16)
    high, low = halves(taps_ref[:16])
    taps_ref[...] = jnp.concatenate([dot(high, flip), dot(low, flip)], axis=0)

    def one(g, carry):
        for j in range(2):
            _, off = base_of(shift_ref[j, g])
            for half in range(2):
                taps = taps_ref[pl.ds(16 * half + 2 * g + j, 1), :]
                taps = pltpu.roll(jnp.broadcast_to(taps, (8, 128)), (129 - off) & 127, 1)
                ring = pltpu.roll(
                    jnp.broadcast_to(taps[:1], (128, 128)), 0, 1, stride=1, stride_axis=0
                )
                for i in range(3):
                    at = lead + (128 * i - off)
                    rows = slice(384 * j + 128 * i, 384 * j + 128 * i + 128)
                    toep[g, rows, 128 * half : 128 * half + 128] = jnp.where(
                        (at >= 0) & (at < 128), ring, 0.0
                    ).astype(BF16)
        return carry

    lax.fori_loop(0, 8, one, 0)


def lens(p, blk, src_ref, shift_ref, ext, toep, lensed_ref):
    for g in range(8):
        wins = []
        for j in range(2):
            which = jnp.clip(src_ref[j, g] - blk + 1, 0, 2)
            base, _ = base_of(shift_ref[j, g])
            for i in range(3):
                rows = pl.ds(8 * g + base + i, 8)
                wins.append(
                    jnp.concatenate([ext[which, l, rows, :] for l in range(NLON)], axis=0)
                )
        high, low = halves(jnp.concatenate(wins, axis=1))
        r = dot(jnp.concatenate([high, low], axis=0), toep[g])
        r = r[:, :128] + r[:, 128:]
        r = r[: 8 * NLON] + r[8 * NLON :]
        for l in range(NLON):
            lensed_ref[l, p // 2, pl.ds(16 * g + p % 2, 8, stride=2), :] = r[8 * l : 8 * l + 8]


def kernel(
    spec_ref, src_hbm, shift_hbm, taps_hbm, first_hbm, cos_hbm, sin_hbm, last_hbm,
    plain_ref, lensed_ref,
    ext_0, ext_1, ext_2, ext_3, land, made, toep, src_ref, shift_ref, taps_ref,
    first_ref, cos_ref, sin_ref, last_ref, first_cat, last_cat,
    own_sem, send_a, recv_a, send_b, recv_b, send_c, recv_c,
):
    ext = (ext_0, ext_1, ext_2, ext_3)
    blk = lax.axis_index("blk")
    lon = lax.axis_index("lon")
    odd = lax.rem(blk, 2)
    near = blk + 1 - 2 * odd
    far = blk - 1 + 2 * odd
    has_far = (blk > 0) & (blk < NBLK - 1)

    barrier = pltpu.get_barrier_semaphore()

    def greet(o, carry):
        pl.semaphore_signal(
            barrier, inc=1, device_id=(lax.rem(blk + o, NBLK), lon), device_id_type=MESH
        )
        return carry

    lax.fori_loop(1, NBLK, greet, 0, unroll=9)
    for d in range(1, NLON):
        pl.semaphore_signal(
            barrier, inc=1, device_id=(blk, lax.rem(lon + d, NLON)), device_id_type=MESH
        )

    @pl.when(has_far)
    def _():
        for d in range(1, NLON):
            pl.semaphore_signal(
                barrier, inc=1, device_id=(far, lax.rem(lon + d, NLON)), device_id_type=MESH
            )

    loads = [
        pltpu.make_async_copy(source, target, own_sem.at[j])
        for j, (source, target) in enumerate(
            [(spec_ref.at[blk, p], land.at[p, blk]) for p in range(PARTS)]
            + [
                (src_hbm, src_ref),
                (shift_hbm, shift_ref),
                (taps_hbm, taps_ref.at[pl.ds(0, 16)]),
                (first_hbm, first_ref),
                (cos_hbm, cos_ref),
                (sin_hbm, sin_ref),
                (last_hbm, last_ref),
            ]
        )
    ]
    for load in loads:
        load.start()
    pl.semaphore_wait(
        barrier, NBLK - 1 + (NLON - 1) * (1 + has_far.astype(jnp.int32))
    )

    def send_spectra(p):
        def one(to):
            pltpu.make_async_remote_copy(
                src_ref=spec_ref.at[to, p],
                dst_ref=land.at[p, blk],
                send_sem=send_a.at[p],
                recv_sem=recv_a.at[p],
                device_id=(to, lon),
                device_id_type=MESH,
            ).start()

        def send(plane, carry):
            @pl.when(plane != blk // 8)
            def _():
                one(8 * plane + lax.rem(blk, 8))

            for step in range(1, 8):
                one(8 * plane + lax.rem(blk + step, 8))
            return carry

        lax.fori_loop(0, NBLK // 8, send, 0)

    def prepare():
        for load in loads:
            load.wait()
        first_cat[...] = jnp.concatenate(halves(first_ref[...]), axis=0)
        for l in range(NLON):
            last_cat[2 * ROWS * l : 2 * ROWS * (l + 1)] = jnp.concatenate(
                halves(last_ref[ROWS * l : ROWS * (l + 1)]), axis=0
            )

    others = [land.at[p, pl.ds(0, NBLK - 1)] for p in range(PARTS)]

    def across(p, d):
        to = lax.rem(lon + d, NLON)
        return pltpu.make_async_remote_copy(
            src_ref=made.at[p, to],
            dst_ref=ext[p].at[1, lon],
            send_sem=send_b,
            recv_sem=recv_b.at[p, d],
            device_id=(blk, to),
            device_id_type=MESH,
        )

    def beside(p, source, l, row, to, slot, side):
        pltpu.make_async_remote_copy(
            src_ref=source,
            dst_ref=ext[p].at[slot, l],
            send_sem=send_c.at[side, p],
            recv_sem=recv_c.at[side, p],
            device_id=(row, to),
            device_id_type=MESH,
        ).start()

    def to_near(p, source, l):
        beside(p, source, l, near, lon, 2 * odd, 0)

    def to_far(p, source, l, to):
        @pl.when(has_far)
        def _():
            beside(p, source, l, far, to, 2 - 2 * odd, 1)

    def keep(p):
        return pltpu.make_async_copy(made.at[p, lon], ext[p].at[1, lon], own_sem.at[11 + p])

    def turn(p):
        pltpu.make_async_copy(others[p], others[p], recv_a.at[p]).wait()
        turned = transform(p, land, first_cat, cos_ref, sin_ref)
        for d in (1, 3, 2, 0):
            to = lax.rem(lon + d, NLON)
            made[p, to] = pixels(last_cat, to, turned)
            if d != 0:
                across(p, d).start()
            if d == 0 or p >= DIRECT:
                to_far(p, made.at[p, to], lon, to)
        to_near(p, made.at[p, lon], lon)
        keep(p).start()

    def pass_on(p):
        for d in (1, 3, 2):
            l = lax.rem(lon + NLON - d, NLON)
            across(p, d).wait_recv()
            to_near(p, ext[p].at[1, l], l)
            if p < DIRECT:
                to_far(p, ext[p].at[1, l], l, lon)

    def finish_part(p):
        keep(p).wait()
        for l in range(NLON):
            plain_ref[l, p // 2, pl.ds(p % 2, 64, stride=2), :] = ext[p][1, l, 4:68, :]
        rows = ext[p].at[0]
        pltpu.make_async_copy(rows, rows, recv_c.at[0, p]).wait()

        @pl.when(has_far)
        def _():
            pltpu.make_async_copy(rows, rows, recv_c.at[1, p]).wait()

        lens(p, blk, src_ref, shift_ref, ext[p], toep, lensed_ref)

    def sent(p):
        rows = ext[p].at[0]
        pltpu.make_async_copy(rows, rows, send_c.at[0, p]).wait()

        @pl.when(has_far)
        def _():
            pltpu.make_async_copy(rows, rows, send_c.at[1, p]).wait()

        pltpu.make_async_copy(others[p], others[p], send_a.at[p]).wait()

    for p in range(PARTS):
        send_spectra(p)
    prepare()
    place_taps(shift_ref, taps_ref, toep)
    turn(0)
    turn(1)
    pass_on(0)
    turn(2)
    pass_on(1)
    turn(3)
    finish_part(0)
    finish_part(1)
    pass_on(2)
    pass_on(3)
    finish_part(2)
    for p in range(3):
        sent(p)
    every = made.at[:, pl.ds(0, NLON - 1)]
    pltpu.make_async_copy(every, every, send_b).wait()
    finish_part(3)
    sent(3)


def finish(plain_vmem, lensed_vmem, plain_ref, lensed_ref, sems):
    copies = [
        pltpu.make_async_copy(source.at[l], target.at[l], sems.at[j, l])
        for j, (source, target) in enumerate(((plain_vmem, plain_ref), (lensed_vmem, lensed_ref)))
        for l in range(NLON)
    ]
    for copy in copies:
        copy.start()
    for copy in copies:
        copy.wait()


def shards(spectra, source_tiles, tap_shift, kernels):
    spec = spectra.reshape(NBLK, 2, 2, 2, 2, 128).transpose(0, 1, 2, 4, 3, 5)
    operands = (
        spec.reshape(NBLK, PARTS, 4, 128),
        source_tiles.transpose(0, 2, 1).reshape(2, 8),
        tap_shift.transpose(0, 2, 1).reshape(2, 8),
        kernels.reshape(16, 128),
        *map(jnp.asarray, tables()),
    )
    vmem = pl.BlockSpec(memory_space=pltpu.VMEM)
    hbm = pl.BlockSpec(memory_space=pltpu.HBM)
    dma = pltpu.SemaphoreType.DMA
    shape = jax.ShapeDtypeStruct((NLON, 2, 128, 128), F32)
    maps_in_vmem = pl.pallas_call(
        kernel,
        out_shape=(shape, shape),
        in_specs=[hbm] * 8,
        out_specs=(vmem, vmem),
        scratch_shapes=[pltpu.VMEM((3, NLON, ROWS, 128), F32)] * PARTS
        + [
            pltpu.VMEM((PARTS, NBLK, 4, 128), F32),
            pltpu.VMEM((PARTS, NLON, ROWS, 128), F32),
            pltpu.VMEM((8, 768, 256), BF16),
            pltpu.SMEM((2, 8), jnp.int32),
            pltpu.SMEM((2, 8), jnp.int32),
            pltpu.VMEM((32, 128), F32),
            pltpu.VMEM((512, 256), F32),
            pltpu.VMEM((128, 256), F32),
            pltpu.VMEM((128, 256), F32),
            pltpu.VMEM((NLON * ROWS, 512), F32),
            pltpu.VMEM((1024, 256), BF16),
            pltpu.VMEM((2 * NLON * ROWS, 512), BF16),
            dma((11 + PARTS,)),
            dma((PARTS,)),
            dma((PARTS,)),
            dma,
            dma((PARTS, NLON)),
            dma((2, PARTS)),
            dma((2, PARTS)),
        ],
        compiler_params=pltpu.CompilerParams(
            collective_id=0, has_side_effects=True, vmem_limit_bytes=32 * 1024 * 1024
        ),
    )(*(pltpu.with_memory_space_constraint(x, pltpu.HBM) for x in operands))
    plain, lensed = pl.pallas_call(
        finish,
        out_shape=(shape, shape),
        in_specs=[vmem, vmem],
        out_specs=(hbm, hbm),
        scratch_shapes=[dma((2, NLON))],
        compiler_params=pltpu.CompilerParams(vmem_limit_bytes=16 * 1024 * 1024),
    )(*maps_in_vmem)

    def maps(x):
        return x.reshape(8, 64, 2, 128).transpose(0, 2, 1, 3).reshape(8, 2, 8192)

    return maps(plain), maps(lensed)


def solution(mesh):
    placed = (
        P(None, "lon", None, None, None, "blk"),
        P("blk", "lon", None),
        P("blk", "lon", None),
        P("blk", "lon", None, None),
    )
    return jax.shard_map(
        shards,
        mesh=mesh,
        in_specs=placed,
        out_specs=(P("blk", None, "lon"), P("blk", None, "lon")),
        check_vma=False,
    )
```
